512 devices in a mesh: dp: 2 (over y_hi), row: 16 (over z, core), col: 16 (over x, y_lo).
Axes of the slice: x: 4, y: 8 (y_hi: 2, y_lo: 4; y = y_hi * 4 + y_lo), z: 8, core: 2. Of those that a mesh axis runs over, the one named last changes fastest.
Arguments:
- inputs: bfloat16 [4096, 6144], P(('dp', 'row'), 'col'), may hold values from -6 to 6
- gain: float32 [6144], P('row'), may hold values from 0.4 to 1.6
- w_in: bfloat16 [6144, 24576], P('row', 'col'), may hold values from -0.078125 to 0.078125
- pre_act: bfloat16 [4096, 24576], P(('dp', 'row'), 'col'), may hold values from -6 to 6
- grad_act: bfloat16 [4096, 24576], P(('dp', 'row'), 'col'), may hold values from -6 to 6
Outputs:
- grad_input: bfloat16 [4096, 6144], P(('dp', 'col'), 'row')
- grad_w_in: float32 [6144, 24576], P('row', 'col')
- grad_gain: float32 [6144], P('row')
The draws below stay inside these ranges and needn't reach their ends.
All inputs are finite; a program needn't handle non-finite values.
Results may differ from the reference program's by a relative error of at most 0.0049.
Values may be sent and summed in bfloat16 or wider, within the bound.
A program may use at most 64 MiB of HBM per device.

```python
import math
import jax
import jax.numpy as jnp
from jax import lax

D = 6144
FF = 24576
TOKENS = 4096


def block_scale(own_key, shape, pieces, least, top_value):
    def one(position, blocks):
        heights = jax.random.uniform(jax.random.fold_in(jax.random.fold_in(own_key, 6), position), (blocks,), jnp.float32, least / len(pieces), top_value / len(pieces))
        return jnp.repeat(jnp.exp(heights), shape[position] // blocks).reshape((-1,) + (1,) * (len(shape) - position - 1))

    level = one(*pieces[0])
    for cut in pieces[1:]:
        level = level * one(*cut)
    return level


def normal_values(own_key, dims, spread, most, pieces=(), kind=jnp.bfloat16):
    factor_of = block_scale(own_key, dims, pieces, -0.22, 0.18) if pieces else 1.0
    values = jax.random.normal(own_key, dims, jnp.float32) * spread * factor_of
    return jnp.minimum(jnp.maximum(values, -most), most).astype(kind)


def setup_inputs(seed: int = 0) -> dict:
    arg_keys = jax.random.split(jax.random.key(seed), 6)
    inputs = normal_values(arg_keys[0], (TOKENS, D), 1.0, 6.0, ((0, 32), (1, 16)))
    gain = jnp.clip(1.0 + 0.12 * jax.random.normal(arg_keys[1], (D,), jnp.float32), 0.4, 1.6)
    w_in = normal_values(arg_keys[2], (D, FF), D ** -0.5, 0.078125, ((0, 16), (1, 16)))
    pre_act = normal_values(arg_keys[3], (TOKENS, FF), 1.5, 6.0, ((0, 32), (1, 16)))
    grad_act = normal_values(arg_keys[4], (TOKENS, FF), 1.0, 6.0, ((0, 32), (1, 16)))
    return dict(inputs=inputs, gain=gain, w_in=w_in, pre_act=pre_act, grad_act=grad_act)


epsilon = 1e-06

def gelu_slope(values):
    coeff = math.sqrt(2.0 / math.pi)
    inner = coeff * (values + 0.044715 * values * values * values)
    tangent = jnp.tanh(inner)
    return 0.5 * (1.0 + tangent) + 0.5 * values * (1.0 - tangent * tangent) * coeff * (1.0 + 3.0 * 0.044715 * values * values)

def reference(inputs, gain, w_in, pre_act, grad_act):
    values = inputs.astype(jnp.float32)
    row_mean = lax.optimization_barrier(jnp.mean(values, axis=1))
    variance = lax.optimization_barrier(jnp.mean(values * values, axis=1)) - row_mean * row_mean
    inv_std = lax.rsqrt(variance + epsilon)
    normed = (values - row_mean[:, None]) * inv_std[:, None]
    hidden = (normed * gain[None, :]).astype(jnp.bfloat16)
    act_grad = (grad_act.astype(jnp.float32) * gelu_slope(pre_act.astype(jnp.float32))).astype(jnp.bfloat16)
    grad_w_in = jnp.dot(hidden.T, act_grad, preferred_element_type=jnp.float32)
    grad_hidden = jnp.dot(act_grad, w_in.T, preferred_element_type=jnp.float32)
    grad_gain = lax.optimization_barrier(jnp.sum(grad_hidden * normed, axis=0))
    scaled = grad_hidden * gain[None, :]
    first_mean = lax.optimization_barrier(jnp.mean(scaled, axis=1))
    second_mean = lax.optimization_barrier(jnp.mean(scaled * normed, axis=1))
    grad_input = (inv_std[:, None] * (scaled - first_mean[:, None] - normed * second_mean[:, None])).astype(jnp.bfloat16)
    return (grad_input, grad_w_in, grad_gain)
```

```python
import math

import jax
import jax.numpy as jnp
from jax import lax
from jax.experimental import pallas as pl
from jax.experimental.pallas import tpu as pltpu
from jax.sharding import PartitionSpec as P

MESH = pl.DeviceIdType.MESH
EPSILON = 1e-06
ROWS = 128
FEAT = 384
UNITS = 1536
NZ, NX, NY = 8, 4, 8
FEATURES = 6144.0
CH = 2
CROWS = ROWS // CH
F32 = jnp.float32
BF16 = jnp.bfloat16
HIGH = lax.Precision.HIGHEST


def gelu_slope(values):
    coeff = math.sqrt(2.0 / math.pi)
    inner = coeff * (values + 0.044715 * values * values * values)
    tangent = jnp.tanh(inner)
    return 0.5 * (1.0 + tangent) + 0.5 * values * (1.0 - tangent * tangent) * coeff * (
        1.0 + 3.0 * 0.044715 * values * values
    )


def kernel(
    x_ref, gain_ref, w_ref, pre_ref, ga_ref,
    gi_ref, gw_ref, gg_ref,
    act, hid, acc, wt, part, rx, own, ty, ry, xin, normed, st1, st2, gy, gx,
    xt_send, xt_recv, act_recv, ring_send, sib_send, dp_send,
    h_recv, hy_send, hx_send, s1_send, s1_recv, s2_send, s2_recv,
    rx_send, rx_recv, ry_send, ry_recv, gy_send, gy_recv, gx_send, gx_recv,
):
    d, r, c = lax.axis_index("dp"), lax.axis_index("row"), lax.axis_index("col")
    z, k = r // 2, r % 2
    x, y = c // 4, c % 4
    yy = d * 4 + y

    def at(dp=None, row=None, col=None):
        return {
            "dp": d if dp is None else dp,
            "row": r if row is None else row,
            "col": c if col is None else col,
        }

    def at_z(zz):
        return at(row=zz * 2 + k)

    def at_y(big):
        return at(dp=big // 4, col=x * 4 + big % 4)

    def at_x(xx):
        return at(col=xx * 4 + y)

    def remote(src, dst, send, recv, device):
        return pltpu.make_async_remote_copy(
            src_ref=src, dst_ref=dst, send_sem=send, recv_sem=recv,
            device_id=device, device_id_type=MESH,
        )

    sibling = at(row=z * 2 + 1 - k)
    zm = lambda s: (z + s + NZ) % NZ
    ym = lambda s: (yy + s + NY) % NY
    xm = lambda s: (x + s + NX) % NX

    barrier = pltpu.get_barrier_semaphore()

    def greet(device):
        pl.semaphore_signal(barrier, inc=1, device_id=device, device_id_type=MESH)

    @pl.loop(1, 16)
    def _(i):
        greet(at(row=(r + i) % 16))

    @pl.loop(1, NY)
    def _(i):
        greet(at_y((yy + i) % NY))

    @pl.loop(1, NX)
    def _(i):
        greet(at_x((x + i) % NX))

    @pl.when(r != c)
    def _():
        greet(at(row=c, col=r))

    @pl.when(r != c)
    def _():
        pl.semaphore_wait(barrier, 15 + NY - 1 + NX - 1 + 1)

    @pl.when(r == c)
    def _():
        pl.semaphore_wait(barrier, 15 + NY - 1 + NX - 1)

    swap = remote(x_ref, xin, xt_send, xt_recv, at(row=c, col=r))

    @pl.when(r != c)
    def _():
        swap.start()

    @pl.when(r == c)
    def _():
        xin[...] = x_ref[...]

    def act_piece(ph, zz, kk, ch):
        return act.at[ph, zz, pl.ds(pl.multiple_of(kk * ROWS + ch * CROWS, CROWS), CROWS), :]

    def ring_copy(ph, zz, ch, to, slot):
        piece = act_piece(ph, zz, k, ch)
        return remote(
            piece, piece, ring_send.at[ph, slot, ch], act_recv.at[ph, zz, k, ch], at_z(to)
        )

    def sib_copy(ph, zz, kk, ch, slot):
        piece = act_piece(ph, zz, kk, ch)
        return remote(
            piece, piece, sib_send.at[ph, slot, ch], act_recv.at[ph, zz, kk, ch], sibling
        )

    def dp_copy(ch):
        return remote(
            act_piece(0, z, k, ch), act_piece(1, z, k, ch),
            dp_send.at[ch], act_recv.at[1, z, k, ch], at(dp=1 - d),
        )

    def wait_act(ph, zz, kk, ch):
        sib_copy(ph, zz, kk, ch, 0).wait_recv()

    def start_own(ph, ch):
        ring_copy(ph, z, ch, zm(1), 0).start()
        ring_copy(ph, z, ch, zm(-1), 1).start()
        sib_copy(ph, z, k, ch, 0).start()

    for ch in range(CH):
        @pl.loop(0, CROWS // 16)
        def _(i):
            here = pl.ds(pl.multiple_of(ch * CROWS + i * 16, 16), 16)
            there = pl.ds(pl.multiple_of(k * ROWS + ch * CROWS + i * 16, 16), 16)
            slopes = gelu_slope(pre_ref[here, :].astype(F32))
            act[0, z, there, :] = (ga_ref[here, :].astype(F32) * slopes).astype(BF16)

        start_own(0, ch)
        dp_copy(ch).start()

    def ring_step(ph, s):
        for ch in range(CH):
            if s < 4:
                for sign, slot in ((-1, 0), (1, 1)):
                    zz = zm(sign * s)
                    wait_act(ph, zz, k, ch)
                    if s < 3:
                        ring_copy(ph, zz, ch, zm(-sign), 2 * s + slot).start()
                    sib_copy(ph, zz, k, ch, 2 * s - 1 + slot).start()
                if s == 3:
                    sign = 2 * k - 1
                    ring_copy(ph, zm(sign * 3), ch, zm(-sign), 6).start()
            else:
                zz = zm(4)
                wait_act(ph, zz, k, ch)
                sib_copy(ph, zz, k, ch, 7).start()

    def wait_sibling(ph, zz):
        for ch in range(CH):
            wait_act(ph, zz, 1 - k, ch)

    @pl.when(r != c)
    def _():
        swap.wait_recv()

    ones = jnp.ones((8, FEAT), F32)
    first_row = lax.broadcasted_iota(jnp.int32, (8, ROWS), 0) == 0

    def row_pair(a, b):
        dims = (((1,), (1,)), ((), ()))
        sum_a = lax.dot_general(ones, a, dims, precision=HIGH, preferred_element_type=F32)
        sum_b = lax.dot_general(ones, b, dims, precision=HIGH, preferred_element_type=F32)
        return jnp.where(first_row, sum_a, sum_b)

    def stat_copy(buf, send, recv, i):
        return remote(buf.at[r], buf.at[r], send.at[i], recv.at[r], at(row=(r + i) % 16))

    def stat_start(buf, send, recv):
        @pl.loop(1, 16)
        def _(i):
            stat_copy(buf, send, recv, i).start()

    def stat_finish(buf, send, recv):
        @pl.loop(1, 16)
        def _(i):
            other = (r + i) % 16
            remote(buf.at[other], buf.at[other], send.at[i], recv.at[other], sibling).wait_recv()

        total = buf[0]
        for i in range(1, 16):
            total = total + buf[i]
        column = jnp.concatenate([total] * 16, axis=0).T / FEATURES
        return column[:, 0:1], column[:, 1:2]

    values = xin[...].astype(F32)
    st1[r] = row_pair(values, values * values)
    stat_start(st1, s1_send, s1_recv)

    @pl.loop(0, UNITS // 128)
    def _(i):
        span = pl.ds(pl.multiple_of(i * 128, 128), 128)
        wt[span, :] = w_ref[:, span].T

    def grad_hidden_part(zz):
        wait_sibling(0, zz)
        half = pl.ds(pl.multiple_of((zz % 2) * 256, 256), 256)
        part[zz // 2, half, :] = jnp.dot(
            act[0, zz], wt[...], preferred_element_type=F32
        ).astype(BF16)

    grad_hidden_part(z)

    row_mean, square_mean = stat_finish(st1, s1_send, s1_recv)
    variance = square_mean - row_mean * row_mean
    inv_std = lax.rsqrt(variance + EPSILON)
    normed[...] = (values - row_mean) * inv_std
    hidden = normed[...] * gain_ref[...]
    hid[d * 16 + c] = hidden.T.astype(BF16)

    def hid_copy(block, device, send):
        return remote(hid.at[block], hid.at[block], send, h_recv.at[block], device)

    def hid_block(big, xx):
        return (big // 4) * 16 + xx * 4 + big % 4

    def hid_to_x(big, slot):
        block = hid_block(big, x)
        hid_copy(block, at_x(xm(1)), hx_send.at[3 * slot]).start()
        hid_copy(block, at_x(xm(-1)), hx_send.at[3 * slot + 1]).start()

    def wait_hid(block):
        hid_copy(block, sibling, hx_send.at[0]).wait_recv()

    def hid_y_step(s):
        if s < 4:
            for sign, slot in ((-1, 0), (1, 1)):
                big = ym(sign * s)
                wait_hid(hid_block(big, x))
                if s < 3:
                    hid_copy(hid_block(big, x), at_y(ym(-sign)), hy_send.at[2 * s + slot]).start()
                hid_to_x(big, 2 * s - 1 + slot)
            if s == 3:
                sign = 2 * k - 1
                hid_copy(hid_block(ym(3 * sign), x), at_y(ym(-sign)), hy_send.at[6]).start()
        else:
            big = ym(4)
            wait_hid(hid_block(big, x))
            hid_to_x(big, 7)

    def y_of(slot):
        if slot == 0:
            return yy
        if slot == 7:
            return ym(4)
        return ym((1, -1)[slot % 2] * ((slot + 1) // 2))

    def hid_x_step(slot):
        big = y_of(slot)
        wait_hid(hid_block(big, xm(1)))
        wait_hid(hid_block(big, xm(-1)))
        sign = 2 * k - 1
        hid_copy(hid_block(big, xm(sign)), at_x(xm(-sign)), hx_send.at[3 * slot + 2]).start()

    for sign, slot in ((1, 0), (-1, 1)):
        hid_copy(hid_block(yy, x), at_y(ym(sign)), hy_send.at[slot]).start()
    hid_to_x(yy, 0)

    def rx_copy(j, i):
        return remote(part.at[j], rx.at[x], rx_send.at[i], rx_recv.at[x], at_x(j))

    def rx_start(j, i):
        @pl.when(j != x)
        def _():
            rx_copy(j, i).start()

    even = 1 - z % 2
    group = (
        z // 2,
        (z // 2 + 4 + 1 - 2 * even) % 4,
        (z // 2 + 4 - 1 + 2 * even) % 4,
        (z // 2 + 2) % 4,
    )

    ring_step(0, 1)
    hid_y_step(1)
    grad_hidden_part(zm(1))
    hid_y_step(2)
    grad_hidden_part(zm(-1))
    rx_start(group[0], 0)
    hid_x_step(0)

    ring_step(0, 2)
    hid_y_step(3)
    hid_x_step(1)
    hid_x_step(2)
    grad_hidden_part(zm(2))
    hid_y_step(4)
    grad_hidden_part(zm(-2))
    rx_start(group[1], 1)
    hid_x_step(3)
    hid_x_step(4)

    ring_step(0, 3)
    for ch in range(CH):
        wait_act(1, z, k, ch)
        start_own(1, ch)
    grad_hidden_part(zm(3))
    hid_x_step(5)
    grad_hidden_part(zm(-3))
    rx_start(group[2], 2)
    hid_x_step(6)
    hid_x_step(7)

    ring_step(0, 4)
    grad_hidden_part(zm(4))
    rx_start(group[3], 3)

    def project(ph, zz, first=False):
        replica = d if ph == 0 else 1 - d
        lhs = jnp.concatenate(
            [hid[replica * 16 + 2 * zz], hid[replica * 16 + 2 * zz + 1]], axis=1
        )

        @pl.loop(0, UNITS // 512)
        def _(i):
            span = pl.ds(pl.multiple_of(i * 512, 512), 512)
            term = jnp.dot(lhs, act[ph, zz, :, span], preferred_element_type=F32)
            out = gw_ref if ph == 0 else acc
            if first:
                out[:, span] = term
            else:
                out[:, span] = out[:, span] + term

    @pl.loop(0, 8)
    def _(slot):
        big = (yy + slot) % NY
        wait_hid(hid_block(big, xm(2)))

    for s in (0, 1, -1, 2):
        project(0, zm(s), first=s == 0)

    ring_step(1, 1)

    for s in (-2, 3, -3, 4):
        project(0, zm(s))

    @pl.loop(1, NX)
    def _(i):
        other = (x + i) % NX
        remote(part.at[0], rx.at[other], rx_send.at[0], rx_recv.at[other], sibling).wait_recv()

    def x_sum(yq):
        rows = pl.ds(pl.multiple_of(yq * ROWS, ROWS), ROWS)
        total = part[x, rows, :].astype(F32)
        for i in range(1, NX):
            total = total + rx[xm(i), rows, :].astype(F32)
        return total

    def ry_copy(i):
        to = (y + i) % 4
        return remote(ty.at[to], ry.at[y], ry_send.at[i], ry_recv.at[y], at(col=x * 4 + to))

    for i in range(1, 4):
        ty[(y + i) % 4] = x_sum((y + i) % 4).astype(BF16)
        ry_copy(i).start()
    own[...] = x_sum(y)

    wait_sibling(1, z)
    project(1, z, first=True)
    ring_step(1, 2)

    for i in range(1, 4):
        other = (y + i) % 4
        remote(ty.at[0], ry.at[other], ry_send.at[0], ry_recv.at[other], sibling).wait_recv()
    grad_hidden = own[...]
    for i in range(1, 4):
        grad_hidden = grad_hidden + ry[(y + i) % 4].astype(F32)

    scaled = grad_hidden * gain_ref[...]
    own_normed = normed[...]
    st2[r] = row_pair(scaled, scaled * own_normed)
    stat_start(st2, s2_send, s2_recv)
    own[...] = scaled

    def gain_sum(buf, count, me, send, recv, device_of):
        @pl.loop(1, count)
        def _(i):
            remote(buf.at[me], buf.at[me], send.at[i], recv.at[me], device_of((me + i) % count)).start()

    def gain_wait(buf, count, me, send, recv):
        @pl.loop(1, count)
        def _(i):
            other = (me + i) % count
            remote(buf.at[other], buf.at[other], send.at[i], recv.at[other], sibling).wait_recv()

        total = buf[0]
        for i in range(1, count):
            total = total + buf[i]
        return total

    def gain_drain(buf, count, me, send, recv):
        @pl.loop(1, count)
        def _(i):
            remote(buf.at[me], buf.at[me], send.at[i], recv.at[me], sibling).wait_send()

    gy[yy] = jnp.broadcast_to(
        jnp.sum(grad_hidden * own_normed, axis=0, keepdims=True), (8, FEAT)
    )
    gain_sum(gy, NY, yy, gy_send, gy_recv, at_y)

    for s in (1, -1):
        wait_sibling(1, zm(s))
        project(1, zm(s))

    gx[x] = gain_wait(gy, NY, yy, gy_send, gy_recv)
    gain_sum(gx, NX, x, gx_send, gx_recv, at_x)
    ring_step(1, 3)

    first_mean, second_mean = stat_finish(st2, s2_send, s2_recv)
    gi_ref[...] = (
        inv_std * (own[...] - first_mean - normed[...] * second_mean)
    ).astype(BF16)

    for s in (2, -2):
        wait_sibling(1, zm(s))
        project(1, zm(s))
    gg_ref[...] = gain_wait(gx, NX, x, gx_send, gx_recv)[0:1, :]
    for s in (3, -3):
        wait_sibling(1, zm(s))
        project(1, zm(s))
    ring_step(1, 4)
    wait_sibling(1, zm(4))
    project(1, zm(4))

    @pl.loop(0, UNITS // 512)
    def _(i):
        span = pl.ds(pl.multiple_of(i * 512, 512), 512)
        gw_ref[:, span] = gw_ref[:, span] + acc[:, span]

    @pl.when(r != c)
    def _():
        swap.wait_send()

    for ch in range(CH):
        dp_copy(ch).wait_send()

    for ph in range(2):
        @pl.loop(0, 7)
        def _(slot):
            for ch in range(CH):
                remote(
                    act_piece(ph, z, k, ch), act_piece(ph, z, k, ch),
                    ring_send.at[ph, slot, ch], act_recv.at[ph, z, k, ch], sibling,
                ).wait_send()

        @pl.loop(0, 8)
        def _(slot):
            for ch in range(CH):
                sib_copy(ph, z, k, ch, slot).wait_send()

    @pl.loop(0, 7)
    def _(slot):
        hid_copy(0, sibling, hy_send.at[slot]).wait_send()

    @pl.loop(0, 24)
    def _(slot):
        hid_copy(0, sibling, hx_send.at[slot]).wait_send()

    for i in range(4):
        @pl.when(group[i] != x)
        def _():
            rx_copy(group[i], i).wait_send()

    for i in range(1, 4):
        ry_copy(i).wait_send()

    for buf, send, recv in ((st1, s1_send, s1_recv), (st2, s2_send, s2_recv)):
        @pl.loop(1, 16)
        def _(i):
            stat_copy(buf, send, recv, i).wait_send()

    gain_drain(gy, NY, yy, gy_send, gy_recv)
    gain_drain(gx, NX, x, gx_send, gx_recv)


def shards(inputs, gain, w_in, pre_act, grad_act):
    dma = pltpu.SemaphoreType.DMA
    grad_input, grad_w_in, grad_gain = pl.pallas_call(
        kernel,
        out_shape=(
            jax.ShapeDtypeStruct((ROWS, FEAT), BF16),
            jax.ShapeDtypeStruct((FEAT, UNITS), F32),
            jax.ShapeDtypeStruct((1, FEAT), F32),
        ),
        in_specs=[pl.BlockSpec(memory_space=pltpu.VMEM)] * 5,
        out_specs=(pl.BlockSpec(memory_space=pltpu.VMEM),) * 3,
        scratch_shapes=[
            pltpu.VMEM((2, NZ, 2 * ROWS, UNITS), BF16),
            pltpu.VMEM((32, FEAT, ROWS), BF16),
            pltpu.VMEM((FEAT, UNITS), F32),
            pltpu.VMEM((UNITS, FEAT), BF16),
            pltpu.VMEM((NX, 4 * ROWS, FEAT), BF16),
            pltpu.VMEM((NX, 4 * ROWS, FEAT), BF16),
            pltpu.VMEM((ROWS, FEAT), F32),
            pltpu.VMEM((4, ROWS, FEAT), BF16),
            pltpu.VMEM((4, ROWS, FEAT), BF16),
            pltpu.VMEM((ROWS, FEAT), BF16),
            pltpu.VMEM((ROWS, FEAT), F32),
            pltpu.VMEM((16, 8, ROWS), F32),
            pltpu.VMEM((16, 8, ROWS), F32),
            pltpu.VMEM((NY, 8, FEAT), F32),
            pltpu.VMEM((NX, 8, FEAT), F32),
            dma, dma, dma((2, NZ, 2, CH)), dma((2, 7, CH)), dma((2, 8, CH)), dma((CH,)),
            dma((32,)), dma((7,)), dma((24,)), dma((16,)), dma((16,)), dma((16,)), dma((16,)),
            dma((4,)), dma((4,)), dma((4,)), dma((4,)), dma((NY,)), dma((NY,)), dma((NX,)), dma((NX,)),
        ],
        compiler_params=pltpu.CompilerParams(
            collective_id=0, has_side_effects=True, vmem_limit_bytes=56 * 1024 * 1024
        ),
    )(inputs, gain.reshape(1, FEAT), w_in, pre_act, grad_act)
    return grad_input, grad_w_in, grad_gain.reshape(FEAT)


def solution(mesh):
    return jax.shard_map(
        shards,
        mesh=mesh,
        in_specs=(
            P(("dp", "row"), "col"),
            P("row"),
            P("row", "col"),
            P(("dp", "row"), "col"),
            P(("dp", "row"), "col"),
        ),
        out_specs=(P(("dp", "col"), "row"), P("row", "col"), P("row")),
        check_vma=False,
    )
```

```python
import math

import jax
import jax.numpy as jnp
from jax import lax
from jax.experimental import pallas as pl
from jax.experimental.pallas import tpu as pltpu
from jax.sharding import PartitionSpec as P

MESH = pl.DeviceIdType.MESH
EPSILON = 1e-06
ROWS = 128
FEAT = 384
UNITS = 1536
NZ, NX, NY = 8, 4, 8
FEATURES = 6144.0
CH = 2
CROWS = ROWS // CH
F32 = jnp.float32
BF16 = jnp.bfloat16
HIGH = lax.Precision.HIGHEST


def gelu_slope(values):
    coeff = math.sqrt(2.0 / math.pi)
    inner = coeff * (values + 0.044715 * values * values * values)
    tangent = jnp.tanh(inner)
    return 0.5 * (1.0 + tangent) + 0.5 * values * (1.0 - tangent * tangent) * coeff * (
        1.0 + 3.0 * 0.044715 * values * values
    )


def kernel(
    x_ref, gain_ref, w_ref, pre_ref, ga_ref,
    gi_ref, gw_ref, gg_ref,
    act, hid, acc, wt, part, rx, own, ty, ry, xin, normed, st1, st2, gy, gx,
    xt_send, xt_recv, act_recv, ring_send, sib_send, dp_send,
    h_recv, hy_send, hx_send, s1_send, s1_recv, s2_send, s2_recv,
    rx_send, rx_recv, ry_send, ry_recv, gy_send, gy_recv, gx_send, gx_recv,
):
    d, r, c = lax.axis_index("dp"), lax.axis_index("row"), lax.axis_index("col")
    z, k = r // 2, r % 2
    x, y = c // 4, c % 4
    yy = d * 4 + y

    def at(dp=None, row=None, col=None):
        return {
            "dp": d if dp is None else dp,
            "row": r if row is None else row,
            "col": c if col is None else col,
        }

    def at_z(zz):
        return at(row=zz * 2 + k)

    def at_y(big):
        return at(dp=big // 4, col=x * 4 + big % 4)

    def at_x(xx):
        return at(col=xx * 4 + y)

    def remote(src, dst, send, recv, device):
        return pltpu.make_async_remote_copy(
            src_ref=src, dst_ref=dst, send_sem=send, recv_sem=recv,
            device_id=device, device_id_type=MESH,
        )

    sibling = at(row=z * 2 + 1 - k)
    zm = lambda s: (z + s + NZ) % NZ
    ym = lambda s: (yy + s + NY) % NY
    xm = lambda s: (x + s + NX) % NX

    gain = gain_ref[...].reshape(1, FEAT)
    barrier = pltpu.get_barrier_semaphore()

    def greet(device):
        pl.semaphore_signal(barrier, inc=1, device_id=device, device_id_type=MESH)

    @pl.loop(1, 16)
    def _(i):
        greet(at(row=(r + i) % 16))

    @pl.loop(1, NY)
    def _(i):
        greet(at_y((yy + i) % NY))

    @pl.loop(1, NX)
    def _(i):
        greet(at_x((x + i) % NX))

    @pl.when(r != c)
    def _():
        greet(at(row=c, col=r))

    @pl.when(r != c)
    def _():
        pl.semaphore_wait(barrier, 15 + NY - 1 + NX - 1 + 1)

    @pl.when(r == c)
    def _():
        pl.semaphore_wait(barrier, 15 + NY - 1 + NX - 1)

    swap = remote(x_ref, xin, xt_send, xt_recv, at(row=c, col=r))

    @pl.when(r != c)
    def _():
        swap.start()

    @pl.when(r == c)
    def _():
        xin[...] = x_ref[...]

    def act_piece(ph, zz, kk, ch):
        return act.at[ph, zz, pl.ds(pl.multiple_of(kk * ROWS + ch * CROWS, CROWS), CROWS), :]

    def ring_copy(ph, zz, ch, to, slot):
        piece = act_piece(ph, zz, k, ch)
        return remote(
            piece, piece, ring_send.at[ph, slot, ch], act_recv.at[ph, zz, k, ch], at_z(to)
        )

    def sib_copy(ph, zz, kk, ch, slot):
        piece = act_piece(ph, zz, kk, ch)
        return remote(
            piece, piece, sib_send.at[ph, slot, ch], act_recv.at[ph, zz, kk, ch], sibling
        )

    def dp_copy(ch):
        return remote(
            act_piece(0, z, k, ch), act_piece(1, z, k, ch),
            dp_send.at[ch], act_recv.at[1, z, k, ch], at(dp=1 - d),
        )

    def wait_act(ph, zz, kk, ch):
        sib_copy(ph, zz, kk, ch, 0).wait_recv()

    def start_own(ph, ch):
        ring_copy(ph, z, ch, zm(1), 0).start()
        ring_copy(ph, z, ch, zm(-1), 1).start()
        sib_copy(ph, z, k, ch, 0).start()

    for ch in range(CH):
        @pl.loop(0, CROWS // 16)
        def _(i):
            here = pl.ds(pl.multiple_of(ch * CROWS + i * 16, 16), 16)
            there = pl.ds(pl.multiple_of(k * ROWS + ch * CROWS + i * 16, 16), 16)
            slopes = gelu_slope(pre_ref[here, :].astype(F32))
            act[0, z, there, :] = (ga_ref[here, :].astype(F32) * slopes).astype(BF16)

        start_own(0, ch)
        dp_copy(ch).start()

    def ring_step(ph, s, ch):
        if s < 4:
            for sign, slot in ((-1, 0), (1, 1)):
                zz = zm(sign * s)
                wait_act(ph, zz, k, ch)
                if s < 3:
                    ring_copy(ph, zz, ch, zm(-sign), 2 * s + slot).start()
                sib_copy(ph, zz, k, ch, 2 * s - 1 + slot).start()
            if s == 3:
                sign = 2 * k - 1
                ring_copy(ph, zm(sign * 3), ch, zm(-sign), 6).start()
        else:
            zz = zm(4)
            wait_act(ph, zz, k, ch)
            sib_copy(ph, zz, k, ch, 7).start()

    def wait_sibling(ph, zz):
        for ch in range(CH):
            wait_act(ph, zz, 1 - k, ch)

    ones = jnp.ones((8, FEAT), F32)
    first_row = lax.broadcasted_iota(jnp.int32, (8, ROWS), 0) == 0

    def row_pair(a, b):
        dims = (((1,), (1,)), ((), ()))
        sum_a = lax.dot_general(ones, a, dims, precision=HIGH, preferred_element_type=F32)
        sum_b = lax.dot_general(ones, b, dims, precision=HIGH, preferred_element_type=F32)
        return jnp.where(first_row, sum_a, sum_b)

    def stat_copy(buf, send, recv, i):
        return remote(buf.at[r], buf.at[r], send.at[i], recv.at[r], at(row=(r + i) % 16))

    def stat_start(buf, send, recv):
        @pl.loop(1, 16)
        def _(i):
            stat_copy(buf, send, recv, i).start()

    def stat_finish(buf, send, recv):
        @pl.loop(1, 16)
        def _(i):
            other = (r + i) % 16
            remote(buf.at[other], buf.at[other], send.at[i], recv.at[other], sibling).wait_recv()

        total = buf[0]
        for i in range(1, 16):
            total = total + buf[i]
        column = jnp.concatenate([total] * 16, axis=0).T / FEATURES
        return column[:, 0:1], column[:, 1:2]

    @pl.loop(0, UNITS // 128)
    def _(i):
        span = pl.ds(pl.multiple_of(i * 128, 128), 128)
        wt[span, :] = w_ref[:, span].T

    def grad_hidden_part(zz):
        wait_sibling(0, zz)
        half = pl.ds(pl.multiple_of((zz % 2) * 256, 256), 256)
        part[zz // 2, half, :] = jnp.dot(
            act[0, zz], wt[...], preferred_element_type=F32
        ).astype(BF16)

    def hid_copy(block, device, send):
        return remote(hid.at[block], hid.at[block], send, h_recv.at[block], device)

    def hid_block(big, xx):
        return (big // 4) * 16 + xx * 4 + big % 4

    def hid_to_x(big, slot):
        block = hid_block(big, x)
        hid_copy(block, at_x(xm(1)), hx_send.at[3 * slot]).start()
        hid_copy(block, at_x(xm(-1)), hx_send.at[3 * slot + 1]).start()

    def wait_hid(block):
        hid_copy(block, sibling, hx_send.at[0]).wait_recv()

    def hid_y_step(s):
        if s < 4:
            for sign, slot in ((-1, 0), (1, 1)):
                big = ym(sign * s)
                wait_hid(hid_block(big, x))
                if s < 3:
                    hid_copy(hid_block(big, x), at_y(ym(-sign)), hy_send.at[2 * s + slot]).start()
                hid_to_x(big, 2 * s - 1 + slot)
            if s == 3:
                sign = 2 * k - 1
                hid_copy(hid_block(ym(3 * sign), x), at_y(ym(-sign)), hy_send.at[6]).start()
        else:
            big = ym(4)
            wait_hid(hid_block(big, x))
            hid_to_x(big, 7)

    def y_of(slot):
        if slot == 0:
            return yy
        if slot == 7:
            return ym(4)
        return ym((1, -1)[slot % 2] * ((slot + 1) // 2))

    def hid_x_step(slot):
        big = y_of(slot)
        wait_hid(hid_block(big, xm(1)))
        wait_hid(hid_block(big, xm(-1)))
        sign = 2 * k - 1
        hid_copy(hid_block(big, xm(sign)), at_x(xm(-sign)), hx_send.at[3 * slot + 2]).start()

    def rx_copy(j, i):
        return remote(part.at[j], rx.at[x], rx_send.at[i], rx_recv.at[x], at_x(j))

    def rx_start(j, i):
        @pl.when(j != x)
        def _():
            rx_copy(j, i).start()

    even = 1 - z % 2
    group = (
        z // 2,
        (z // 2 + 4 + 1 - 2 * even) % 4,
        (z // 2 + 4 - 1 + 2 * even) % 4,
        (z // 2 + 2) % 4,
    )

    def project(ph, zz, first=False, last=False):
        replica = d if ph == 0 else 1 - d
        lhs = jnp.concatenate(
            [hid[replica * 16 + 2 * zz], hid[replica * 16 + 2 * zz + 1]], axis=1
        )

        @pl.loop(0, UNITS // 512)
        def _(i):
            span = pl.ds(pl.multiple_of(i * 512, 512), 512)
            term = jnp.dot(lhs, act[ph, zz, :, span], preferred_element_type=F32)
            out = gw_ref if ph == 0 else acc
            if first:
                out[:, span] = term
            elif last:
                gw_ref[:, span] = gw_ref[:, span] + (acc[:, span] + term)
            else:
                out[:, span] = out[:, span] + term

    def x_sum(yq):
        rows = pl.ds(pl.multiple_of(yq * ROWS, ROWS), ROWS)
        total = part[x, rows, :].astype(F32)
        for i in range(1, NX):
            total = total + rx[xm(i), rows, :].astype(F32)
        return total

    def ry_copy(i):
        to = (y + i) % 4
        return remote(ty.at[to], ry.at[y], ry_send.at[i], ry_recv.at[y], at(col=x * 4 + to))

    def gain_sum(buf, count, me, send, recv, device_of):
        @pl.loop(1, count)
        def _(i):
            remote(buf.at[me], buf.at[me], send.at[i], recv.at[me], device_of((me + i) % count)).start()

    def gain_wait(buf, count, me, send, recv):
        @pl.loop(1, count)
        def _(i):
            other = (me + i) % count
            remote(buf.at[other], buf.at[other], send.at[i], recv.at[other], sibling).wait_recv()

        total = buf[0]
        for i in range(1, count):
            total = total + buf[i]
        return total

    def gain_drain(buf, count, me, send, recv):
        @pl.loop(1, count)
        def _(i):
            remote(buf.at[me], buf.at[me], send.at[i], recv.at[me], sibling).wait_send()

    grad_hidden_part(z)
    ring_step(0, 1, 0)

    @pl.when(r != c)
    def _():
        swap.wait_recv()

    values = xin[...].astype(F32)
    st1[r] = row_pair(values, values * values)
    stat_start(st1, s1_send, s1_recv)
    ring_step(0, 1, 1)
    grad_hidden_part(zm(1))
    grad_hidden_part(zm(-1))
    rx_start(group[0], 0)

    row_mean, square_mean = stat_finish(st1, s1_send, s1_recv)
    variance = square_mean - row_mean * row_mean
    inv_std = lax.rsqrt(variance + EPSILON)
    normed[...] = (xin[...].astype(F32) - row_mean) * inv_std
    hid[d * 16 + c] = (normed[...] * gain).T.astype(BF16)
    for sign, slot in ((1, 0), (-1, 1)):
        hid_copy(hid_block(yy, x), at_y(ym(sign)), hy_send.at[slot]).start()
    hid_to_x(yy, 0)

    ring_step(0, 2, 0)
    hid_y_step(1)
    ring_step(0, 2, 1)
    hid_y_step(2)
    hid_x_step(0)
    grad_hidden_part(zm(2))
    grad_hidden_part(zm(-2))
    rx_start(group[1], 1)
    ring_step(0, 3, 0)
    hid_y_step(3)
    hid_x_step(1)
    ring_step(0, 3, 1)
    for ch in range(CH):
        wait_act(1, z, k, ch)
        start_own(1, ch)
    hid_y_step(4)
    hid_x_step(2)
    ring_step(0, 4, 0)
    hid_x_step(3)
    ring_step(0, 4, 1)
    grad_hidden_part(zm(3))
    grad_hidden_part(zm(-3))
    rx_start(group[2], 2)
    grad_hidden_part(zm(4))
    rx_start(group[3], 3)
    hid_x_step(4)
    ring_step(1, 1, 0)
    hid_x_step(5)
    hid_x_step(6)
    hid_x_step(7)
    ring_step(1, 1, 1)

    @pl.loop(1, NX)
    def _(i):
        other = (x + i) % NX
        remote(part.at[0], rx.at[other], rx_send.at[0], rx_recv.at[other], sibling).wait_recv()

    for i in range(1, 4):
        ty[(y + i) % 4] = x_sum((y + i) % 4).astype(BF16)
        ry_copy(i).start()
    own[...] = x_sum(y)
    ring_step(1, 2, 0)

    @pl.loop(0, 8)
    def _(slot):
        big = (yy + slot) % NY
        wait_hid(hid_block(big, xm(2)))

    for s in (0, 1, -1, 2):
        project(0, zm(s), first=s == 0)

    for i in range(1, 4):
        other = (y + i) % 4
        remote(ty.at[0], ry.at[other], ry_send.at[0], ry_recv.at[other], sibling).wait_recv()
    grad_hidden = own[...]
    for i in range(1, 4):
        grad_hidden = grad_hidden + ry[(y + i) % 4].astype(F32)

    scaled = grad_hidden * gain
    own_normed = normed[...]
    st2[r] = row_pair(scaled, scaled * own_normed)
    stat_start(st2, s2_send, s2_recv)
    own[...] = scaled
    gy[yy] = jnp.broadcast_to(
        jnp.sum(grad_hidden * own_normed, axis=0, keepdims=True), (8, FEAT)
    )
    gain_sum(gy, NY, yy, gy_send, gy_recv, at_y)
    ring_step(1, 2, 1)

    for s in (-2, 3, -3, 4):
        project(0, zm(s))

    wait_sibling(1, z)
    project(1, z, first=True)
    ring_step(1, 3, 0)
    gx[x] = gain_wait(gy, NY, yy, gy_send, gy_recv)
    gain_sum(gx, NX, x, gx_send, gx_recv, at_x)

    first_mean, second_mean = stat_finish(st2, s2_send, s2_recv)
    gi_ref[...] = (
        inv_std * (own[...] - first_mean - normed[...] * second_mean)
    ).astype(BF16)
    for s in (1, -1):
        wait_sibling(1, zm(s))
        project(1, zm(s))
    ring_step(1, 3, 1)
    for s in (2, -2):
        wait_sibling(1, zm(s))
        project(1, zm(s))
    gg_ref[...] = gain_wait(gx, NX, x, gx_send, gx_recv)[0]
    ring_step(1, 4, 0)
    for s in (3, -3):
        wait_sibling(1, zm(s))
        project(1, zm(s))
    ring_step(1, 4, 1)
    wait_sibling(1, zm(4))
    project(1, zm(4), last=True)

    @pl.when(r != c)
    def _():
        swap.wait_send()

    for ch in range(CH):
        dp_copy(ch).wait_send()

    for ph in range(2):
        @pl.loop(0, 7)
        def _(slot):
            for ch in range(CH):
                remote(
                    act_piece(ph, z, k, ch), act_piece(ph, z, k, ch),
                    ring_send.at[ph, slot, ch], act_recv.at[ph, z, k, ch], sibling,
                ).wait_send()

        @pl.loop(0, 8)
        def _(slot):
            for ch in range(CH):
                sib_copy(ph, z, k, ch, slot).wait_send()

    @pl.loop(0, 7)
    def _(slot):
        hid_copy(0, sibling, hy_send.at[slot]).wait_send()

    @pl.loop(0, 24)
    def _(slot):
        hid_copy(0, sibling, hx_send.at[slot]).wait_send()

    for i in range(4):
        @pl.when(group[i] != x)
        def _():
            rx_copy(group[i], i).wait_send()

    for i in range(1, 4):
        ry_copy(i).wait_send()

    for buf, send, recv in ((st1, s1_send, s1_recv), (st2, s2_send, s2_recv)):
        @pl.loop(1, 16)
        def _(i):
            stat_copy(buf, send, recv, i).wait_send()

    gain_drain(gy, NY, yy, gy_send, gy_recv)
    gain_drain(gx, NX, x, gx_send, gx_recv)


def shards(inputs, gain, w_in, pre_act, grad_act):
    dma = pltpu.SemaphoreType.DMA
    grad_input, grad_w_in, grad_gain = pl.pallas_call(
        kernel,
        out_shape=(
            jax.ShapeDtypeStruct((ROWS, FEAT), BF16),
            pltpu.VMEM((FEAT, UNITS), F32),
            jax.ShapeDtypeStruct((FEAT,), F32),
        ),
        in_specs=[pl.BlockSpec(memory_space=pltpu.VMEM)] * 5,
        out_specs=(pl.BlockSpec(memory_space=pltpu.VMEM),) * 3,
        scratch_shapes=[
            pltpu.VMEM((2, NZ, 2 * ROWS, UNITS), BF16),
            pltpu.VMEM((32, FEAT, ROWS), BF16),
            pltpu.VMEM((FEAT, UNITS), F32),
            pltpu.VMEM((UNITS, FEAT), BF16),
            pltpu.VMEM((NX, 4 * ROWS, FEAT), BF16),
            pltpu.VMEM((NX, 4 * ROWS, FEAT), BF16),
            pltpu.VMEM((ROWS, FEAT), F32),
            pltpu.VMEM((4, ROWS, FEAT), BF16),
            pltpu.VMEM((4, ROWS, FEAT), BF16),
            pltpu.VMEM((ROWS, FEAT), BF16),
            pltpu.VMEM((ROWS, FEAT), F32),
            pltpu.VMEM((16, 8, ROWS), F32),
            pltpu.VMEM((16, 8, ROWS), F32),
            pltpu.VMEM((NY, 8, FEAT), F32),
            pltpu.VMEM((NX, 8, FEAT), F32),
            dma, dma, dma((2, NZ, 2, CH)), dma((2, 7, CH)), dma((2, 8, CH)), dma((CH,)),
            dma((32,)), dma((7,)), dma((24,)), dma((16,)), dma((16,)), dma((16,)), dma((16,)),
            dma((4,)), dma((4,)), dma((4,)), dma((4,)), dma((NY,)), dma((NY,)), dma((NX,)), dma((NX,)),
        ],
        compiler_params=pltpu.CompilerParams(
            collective_id=0, has_side_effects=True, vmem_limit_bytes=40 * 1024 * 1024
        ),
    )(inputs, gain, w_in, pre_act, grad_act)
    return grad_input, grad_w_in, grad_gain


def solution(mesh):
    return jax.shard_map(
        shards,
        mesh=mesh,
        in_specs=(
            P(("dp", "row"), "col"),
            P("row"),
            P("row", "col"),
            P(("dp", "row"), "col"),
            P(("dp", "row"), "col"),
        ),
        out_specs=(P(("dp", "col"), "row"), P("row", "col"), P("row")),
        check_vma=False,
    )
```

```python
import math

import jax
import jax.numpy as jnp
from jax import lax
from jax.experimental import pallas as pl
from jax.experimental.pallas import tpu as pltpu
from jax.sharding import PartitionSpec as P

MESH = pl.DeviceIdType.MESH
EPSILON = 1e-06
ROWS = 128
FEAT = 384
UNITS = 1536
NZ, NX, NY = 8, 4, 8
FEATURES = 6144.0
CH = 2
CROWS = ROWS // CH
F32 = jnp.float32
BF16 = jnp.bfloat16
HIGH = lax.Precision.HIGHEST


def gelu_slope(values):
    coeff = math.sqrt(2.0 / math.pi)
    inner = coeff * (values + 0.044715 * values * values * values)
    tangent = jnp.tanh(inner)
    return 0.5 * (1.0 + tangent) + 0.5 * values * (1.0 - tangent * tangent) * coeff * (
        1.0 + 3.0 * 0.044715 * values * values
    )


def kernel(
    x_in, gain_in, w_in, pre_in, ga_in,
    gi_ref, gw_ref, gg_ref,
    x_ref, gain_ref, w_ref, pre_ref, ga_ref, load,
    act, hid, acc, wt, part, rx, own, ty, ry, xin, normed, st1, st2, stot, stin, gy, gx,
    xt_send, xt_recv, sin_send, sin_recv, act_recv, ring_send, sib_send, dp_send,
    h_recv, hy_send, hx_send, s1_send, s1_recv, s2_send, s2_recv,
    rx_send, rx_recv, ry_send, ry_recv, gy_send, gy_recv, gx_send, gx_recv,
):
    d, r, c = lax.axis_index("dp"), lax.axis_index("row"), lax.axis_index("col")
    z, k = r // 2, r % 2
    x, y = c // 4, c % 4
    yy = d * 4 + y

    def at(dp=None, row=None, col=None):
        return {
            "dp": d if dp is None else dp,
            "row": r if row is None else row,
            "col": c if col is None else col,
        }

    def at_z(zz):
        return at(row=zz * 2 + k)

    def at_y(big):
        return at(dp=big // 4, col=x * 4 + big % 4)

    def at_x(xx):
        return at(col=xx * 4 + y)

    def remote(src, dst, send, recv, device):
        return pltpu.make_async_remote_copy(
            src_ref=src, dst_ref=dst, send_sem=send, recv_sem=recv,
            device_id=device, device_id_type=MESH,
        )

    sibling = at(row=z * 2 + 1 - k)
    zm = lambda s: (z + s + NZ) % NZ
    ym = lambda s: (yy + s + NY) % NY
    xm = lambda s: (x + s + NX) % NX

    loads = [
        pltpu.make_async_copy(src, dst, load.at[i])
        for i, (src, dst) in enumerate(
            ((pre_in, pre_ref), (ga_in, ga_ref), (x_in, x_ref), (gain_in, gain_ref), (w_in, w_ref))
        )
    ]
    for copy in loads:
        copy.start()

    barrier = pltpu.get_barrier_semaphore()

    def greet(device):
        pl.semaphore_signal(barrier, inc=1, device_id=device, device_id_type=MESH)

    @pl.loop(1, 16)
    def _(i):
        greet(at(row=(r + i) % 16))

    @pl.loop(1, 16)
    def _(i):
        greet(at(col=(c + i) % 16))

    @pl.loop(0, 4)
    def _(i):
        greet(at(dp=1 - d, col=x * 4 + i))

    @pl.when(r != c)
    def _():
        greet(at(row=c, col=r))

    @pl.when(r != c)
    def _():
        pl.semaphore_wait(barrier, 15 + 15 + 4 + 1)

    @pl.when(r == c)
    def _():
        pl.semaphore_wait(barrier, 15 + 15 + 4)

    for copy in loads:
        copy.wait()
    gain = gain_ref[...].reshape(1, FEAT)

    swap = remote(x_ref, xin, xt_send, xt_recv, at(row=c, col=r))

    @pl.when(r != c)
    def _():
        swap.start()

    @pl.when(r == c)
    def _():
        xin[...] = x_ref[...]

    def act_piece(ph, zz, kk, ch):
        return act.at[ph, zz, pl.ds(pl.multiple_of(kk * ROWS + ch * CROWS, CROWS), CROWS), :]

    def ring_copy(ph, zz, ch, to, slot):
        piece = act_piece(ph, zz, k, ch)
        return remote(
            piece, piece, ring_send.at[ph, slot, ch], act_recv.at[ph, zz, k, ch], at_z(to)
        )

    def sib_copy(ph, zz, kk, ch, slot):
        piece = act_piece(ph, zz, kk, ch)
        return remote(
            piece, piece, sib_send.at[ph, slot, ch], act_recv.at[ph, zz, kk, ch], sibling
        )

    def dp_copy(ch):
        return remote(
            act_piece(0, z, k, ch), act_piece(1, z, k, ch),
            dp_send.at[ch], act_recv.at[1, z, k, ch], at(dp=1 - d),
        )

    def wait_act(ph, zz, kk, ch):
        sib_copy(ph, zz, kk, ch, 0).wait_recv()

    def start_own(ph, ch):
        ring_copy(ph, z, ch, zm(1), 0).start()
        ring_copy(ph, z, ch, zm(-1), 1).start()
        sib_copy(ph, z, k, ch, 0).start()

    for ch in range(CH):
        @pl.loop(0, CROWS // 16)
        def _(i):
            here = pl.ds(pl.multiple_of(ch * CROWS + i * 16, 16), 16)
            there = pl.ds(pl.multiple_of(k * ROWS + ch * CROWS + i * 16, 16), 16)
            slopes = gelu_slope(pre_ref[here, :].astype(F32))
            act[0, z, there, :] = (ga_ref[here, :].astype(F32) * slopes).astype(BF16)

        start_own(0, ch)
        if ch == 0:
            dp_copy(ch).start()

    def ring_step(ph, s, ch):
        if s < 4:
            for sign, slot in ((-1, 0), (1, 1)):
                zz = zm(sign * s)
                wait_act(ph, zz, k, ch)
                if s < 3:
                    ring_copy(ph, zz, ch, zm(-sign), 2 * s + slot).start()
                sib_copy(ph, zz, k, ch, 2 * s - 1 + slot).start()
            if s == 3:
                sign = 2 * k - 1
                ring_copy(ph, zm(sign * 3), ch, zm(-sign), 6).start()
        else:
            zz = zm(4)
            wait_act(ph, zz, k, ch)
            sib_copy(ph, zz, k, ch, 7).start()

    def wait_sibling(ph, zz):
        for ch in range(CH):
            wait_act(ph, zz, 1 - k, ch)

    ones = jnp.ones((8, FEAT), F32)
    first_row = lax.broadcasted_iota(jnp.int32, (8, ROWS), 0) == 0

    def row_pair(a, b):
        dims = (((1,), (1,)), ((), ()))
        sum_a = lax.dot_general(ones, a, dims, precision=HIGH, preferred_element_type=F32)
        sum_b = lax.dot_general(ones, b, dims, precision=HIGH, preferred_element_type=F32)
        return jnp.where(first_row, sum_a, sum_b)

    def stat_peer(axis, i):
        return at(row=(r + i) % 16) if axis == "row" else at(col=(c + i) % 16)

    def stat_copy(buf, send, recv, axis, i):
        me = r if axis == "row" else c
        return remote(buf.at[me], buf.at[me], send.at[i], recv.at[me], stat_peer(axis, i))

    def stat_start(buf, send, recv, axis):
        @pl.loop(1, 16)
        def _(i):
            stat_copy(buf, send, recv, axis, i).start()

    def stat_finish(buf, send, recv, axis):
        @pl.loop(1, 16)
        def _(i):
            other = ((r if axis == "row" else c) + i) % 16
            remote(buf.at[other], buf.at[other], send.at[i], recv.at[other], sibling).wait_recv()

        total = buf[0]
        for i in range(1, 16):
            total = total + buf[i]
        return total

    def columns_of(total):
        column = jnp.concatenate([total] * 16, axis=0).T / FEATURES
        return column[:, 0:1], column[:, 1:2]

    values = x_ref[...].astype(F32)
    st1[c] = row_pair(values, values * values)
    stat_start(st1, s1_send, s1_recv, "col")
    total_copy = remote(stot, stin, sin_send, sin_recv, at(row=c, col=r))

    @pl.loop(0, UNITS // 128)
    def _(i):
        span = pl.ds(pl.multiple_of(i * 128, 128), 128)
        wt[span, :] = w_ref[:, span].T

    def rx_copy(zz, i):
        half = pl.ds(pl.multiple_of((zz % 2) * 256, 256), 256)
        return remote(
            part.at[zz], rx.at[x, half], rx_send.at[i], rx_recv.at[x, zz % 2], at_x(zz // 2)
        )

    def grad_hidden_part(s, i):
        zz = zm(s)
        wait_sibling(0, zz)
        part[zz] = jnp.dot(act[0, zz], wt[...], preferred_element_type=F32).astype(BF16)

        @pl.when(zz // 2 != x)
        def _():
            rx_copy(zz, i).start()

    def hid_copy(block, device, send):
        return remote(hid.at[block], hid.at[block], send, h_recv.at[block], device)

    def hid_block(big, xx):
        return (big // 4) * 16 + xx * 4 + big % 4

    def hid_to_x(big):
        block = hid_block(big, x)
        hid_copy(block, at_x(xm(1)), hx_send.at[3 * big]).start()
        hid_copy(block, at_x(xm(-1)), hx_send.at[3 * big + 1]).start()

    def wait_hid(block):
        hid_copy(block, sibling, hx_send.at[0]).wait_recv()

    def hid_arrived(big):
        wait_hid(hid_block(big, x))

        @pl.when(big // 4 == d)
        def _():
            hid_to_x(big)

    def hid_y_step(s):
        if s < 4:
            for sign, slot in ((-1, 0), (1, 1)):
                big = ym(sign * s)
                hid_arrived(big)
                if s < 3:
                    hid_copy(hid_block(big, x), at_y(ym(-sign)), hy_send.at[2 * s + slot]).start()
            if s == 3:
                sign = 2 * k - 1
                hid_copy(hid_block(ym(3 * sign), x), at_y(ym(-sign)), hy_send.at[6]).start()
        else:
            hid_arrived(ym(4))

    def hid_others():
        for i in range(4):
            hid_to_x((1 - d) * 4 + (y + i) % 4)

    def hid_x_step(ph, i):
        big = (d if ph == 0 else 1 - d) * 4 + (y + i) % 4
        wait_hid(hid_block(big, xm(1)))
        wait_hid(hid_block(big, xm(-1)))
        sign = 2 * k - 1
        hid_copy(hid_block(big, xm(sign)), at_x(xm(-sign)), hx_send.at[3 * big + 2]).start()

    def hid_ready(ph):
        @pl.loop(0, 4)
        def _(i):
            wait_hid(hid_block((d if ph == 0 else 1 - d) * 4 + i, xm(2)))

    def project(ph, zz, first=False, last=False):
        replica = d if ph == 0 else 1 - d
        lhs = jnp.concatenate(
            [hid[replica * 16 + 2 * zz], hid[replica * 16 + 2 * zz + 1]], axis=1
        )

        @pl.loop(0, UNITS // 512)
        def _(i):
            span = pl.ds(pl.multiple_of(i * 512, 512), 512)
            term = jnp.dot(lhs, act[ph, zz, :, span], preferred_element_type=F32)
            out = gw_ref if ph == 0 else acc
            if first:
                out[:, span] = term
            elif last:
                gw_ref[:, span] = gw_ref[:, span] + (acc[:, span] + term)
            else:
                out[:, span] = out[:, span] + term

    def x_sum(yq):
        rows = pl.ds(pl.multiple_of(yq * ROWS, ROWS), ROWS)
        inner = pl.ds(pl.multiple_of((yq % 2) * ROWS, ROWS), ROWS)
        total = part[2 * x + yq // 2, inner, :].astype(F32)
        for i in range(1, NX):
            total = total + rx[xm(i), rows, :].astype(F32)
        return total

    def ry_copy(i):
        to = (y + i) % 4
        return remote(ty.at[to], ry.at[y], ry_send.at[i], ry_recv.at[y], at(col=x * 4 + to))

    def gain_sum(buf, count, me, send, recv, device_of):
        @pl.loop(1, count)
        def _(i):
            remote(buf.at[me], buf.at[me], send.at[i], recv.at[me], device_of((me + i) % count)).start()

    def gain_wait(buf, count, me, send, recv):
        @pl.loop(1, count)
        def _(i):
            other = (me + i) % count
            remote(buf.at[other], buf.at[other], send.at[i], recv.at[other], sibling).wait_recv()

        total = buf[0]
        for i in range(1, count):
            total = total + buf[i]
        return total

    def gain_drain(buf, count, me, send, recv):
        @pl.loop(1, count)
        def _(i):
            remote(buf.at[me], buf.at[me], send.at[i], recv.at[me], sibling).wait_send()

    grad_hidden_part(0, 0)
    stot[...] = stat_finish(st1, s1_send, s1_recv, "col")

    @pl.when(r != c)
    def _():
        total_copy.start()

    @pl.when(r == c)
    def _():
        stin[...] = stot[...]

    ring_step(0, 1, 0)
    ring_step(0, 1, 1)

    @pl.when(r != c)
    def _():
        swap.wait_recv()
        total_copy.wait_recv()

    row_mean, square_mean = columns_of(stin[...])
    variance = square_mean - row_mean * row_mean
    inv_std = lax.rsqrt(variance + EPSILON)
    normed[...] = (xin[...].astype(F32) - row_mean) * inv_std
    hid[d * 16 + c] = (normed[...] * gain).T.astype(BF16)
    for sign, slot in ((1, 0), (-1, 1)):
        hid_copy(hid_block(yy, x), at_y(ym(sign)), hy_send.at[slot]).start()
    hid_to_x(yy)
    dp_copy(1).start()

    grad_hidden_part(1, 1)
    grad_hidden_part(-1, 2)
    ring_step(0, 2, 0)
    hid_y_step(1)
    hid_x_step(0, 0)
    ring_step(0, 2, 1)
    grad_hidden_part(2, 3)
    grad_hidden_part(-2, 4)
    hid_y_step(2)
    ring_step(0, 3, 0)
    wait_act(1, z, k, 0)
    start_own(1, 0)
    hid_y_step(3)
    ring_step(0, 3, 1)
    wait_act(1, z, k, 1)
    start_own(1, 1)
    grad_hidden_part(3, 5)
    grad_hidden_part(-3, 6)
    ring_step(0, 4, 0)
    hid_y_step(4)
    hid_x_step(0, 1)
    hid_x_step(0, 2)
    hid_x_step(0, 3)
    ring_step(1, 1, 0)
    ring_step(0, 4, 1)
    grad_hidden_part(4, 7)
    hid_others()
    hid_ready(0)
    ring_step(1, 1, 1)
    for s in (0, 1, -1, 2, -2, 3):
        project(0, zm(s), first=s == 0)
    ring_step(1, 2, 0)

    for half in range(2):
        @pl.loop(1, NX)
        def _(i):
            other = (x + i) % NX
            rows = pl.ds(half * 256, 256)
            remote(
                part.at[0], rx.at[other, rows], rx_send.at[0], rx_recv.at[other, half], sibling
            ).wait_recv()

    for i in range(1, 4):
        ty[(y + i) % 4] = x_sum((y + i) % 4).astype(BF16)
        ry_copy(i).start()
    own[...] = x_sum(y)
    hid_x_step(1, 0)
    hid_x_step(1, 1)
    ring_step(1, 2, 1)
    hid_x_step(1, 2)
    hid_x_step(1, 3)
    for s in (-3, 4):
        project(0, zm(s))
    ring_step(1, 3, 0)

    for i in range(1, 4):
        other = (y + i) % 4
        remote(ty.at[0], ry.at[other], ry_send.at[0], ry_recv.at[other], sibling).wait_recv()
    grad_hidden = own[...]
    for i in range(1, 4):
        grad_hidden = grad_hidden + ry[(y + i) % 4].astype(F32)

    scaled = grad_hidden * gain
    own_normed = normed[...]
    st2[r] = row_pair(scaled, scaled * own_normed)
    stat_start(st2, s2_send, s2_recv, "row")
    own[...] = scaled
    gy[yy] = jnp.broadcast_to(
        jnp.sum(grad_hidden * own_normed, axis=0, keepdims=True), (8, FEAT)
    )
    gain_sum(gy, NY, yy, gy_send, gy_recv, at_y)
    ring_step(1, 3, 1)
    hid_ready(1)
    wait_sibling(1, z)
    project(1, z, first=True)
    for s in (1, -1):
        wait_sibling(1, zm(s))
        project(1, zm(s))
    ring_step(1, 4, 0)
    gx[x] = gain_wait(gy, NY, yy, gy_send, gy_recv)
    gain_sum(gx, NX, x, gx_send, gx_recv, at_x)
    for s in (2, -2):
        wait_sibling(1, zm(s))
        project(1, zm(s))
    first_mean, second_mean = columns_of(stat_finish(st2, s2_send, s2_recv, "row"))
    gi_ref[...] = (
        inv_std * (own[...] - first_mean - normed[...] * second_mean)
    ).astype(BF16)
    ring_step(1, 4, 1)
    for s in (3, -3):
        wait_sibling(1, zm(s))
        project(1, zm(s))
    wait_sibling(1, zm(4))
    project(1, zm(4), last=True)
    gg_ref[...] = gain_wait(gx, NX, x, gx_send, gx_recv)[0]

    @pl.when(r != c)
    def _():
        swap.wait_send()
        total_copy.wait_send()

    for ch in range(CH):
        dp_copy(ch).wait_send()

    for ph in range(2):
        @pl.loop(0, 7)
        def _(slot):
            for ch in range(CH):
                remote(
                    act_piece(ph, z, k, ch), act_piece(ph, z, k, ch),
                    ring_send.at[ph, slot, ch], act_recv.at[ph, z, k, ch], sibling,
                ).wait_send()

        @pl.loop(0, 8)
        def _(slot):
            for ch in range(CH):
                sib_copy(ph, z, k, ch, slot).wait_send()

    @pl.loop(0, 7)
    def _(slot):
        hid_copy(0, sibling, hy_send.at[slot]).wait_send()

    @pl.loop(0, 24)
    def _(slot):
        hid_copy(0, sibling, hx_send.at[slot]).wait_send()

    for i, step in enumerate((0, 1, -1, 2, -2, 3, -3, 4)):
        @pl.when(zm(step) // 2 != x)
        def _():
            rx_copy(zm(step), i).wait_send()

    for i in range(1, 4):
        ry_copy(i).wait_send()

    for buf, send, recv, axis in ((st1, s1_send, s1_recv, "col"), (st2, s2_send, s2_recv, "row")):
        @pl.loop(1, 16)
        def _(i):
            stat_copy(buf, send, recv, axis, i).wait_send()

    gain_drain(gy, NY, yy, gy_send, gy_recv)
    gain_drain(gx, NX, x, gx_send, gx_recv)


def shards(inputs, gain, w_in, pre_act, grad_act):
    dma = pltpu.SemaphoreType.DMA
    grad_input, grad_w_in, grad_gain = pl.pallas_call(
        kernel,
        out_shape=(
            jax.ShapeDtypeStruct((ROWS, FEAT), BF16),
            pltpu.VMEM((FEAT, UNITS), F32),
            jax.ShapeDtypeStruct((FEAT,), F32),
        ),
        in_specs=[pl.BlockSpec(memory_space=pltpu.HBM)] * 5,
        out_specs=(pl.BlockSpec(memory_space=pltpu.VMEM),) * 3,
        scratch_shapes=[
            pltpu.VMEM((ROWS, FEAT), BF16),
            pltpu.VMEM((FEAT,), F32),
            pltpu.VMEM((FEAT, UNITS), BF16),
            pltpu.VMEM((ROWS, UNITS), BF16),
            pltpu.VMEM((ROWS, UNITS), BF16),
            dma((5,)),
            pltpu.VMEM((2, NZ, 2 * ROWS, UNITS), BF16),
            pltpu.VMEM((32, FEAT, ROWS), BF16),
            pltpu.VMEM((FEAT, UNITS), F32),
            pltpu.VMEM((UNITS, FEAT), BF16),
            pltpu.VMEM((NZ, 2 * ROWS, FEAT), BF16),
            pltpu.VMEM((NX, 4 * ROWS, FEAT), BF16),
            pltpu.VMEM((ROWS, FEAT), F32),
            pltpu.VMEM((4, ROWS, FEAT), BF16),
            pltpu.VMEM((4, ROWS, FEAT), BF16),
            pltpu.VMEM((ROWS, FEAT), BF16),
            pltpu.VMEM((ROWS, FEAT), F32),
            pltpu.VMEM((16, 8, ROWS), F32),
            pltpu.VMEM((16, 8, ROWS), F32),
            pltpu.VMEM((8, ROWS), F32),
            pltpu.VMEM((8, ROWS), F32),
            pltpu.VMEM((NY, 8, FEAT), F32),
            pltpu.VMEM((NX, 8, FEAT), F32),
            dma, dma, dma, dma, dma((2, NZ, 2, CH)), dma((2, 7, CH)), dma((2, 8, CH)), dma((CH,)),
            dma((32,)), dma((7,)), dma((24,)), dma((16,)), dma((16,)), dma((16,)), dma((16,)),
            dma((8,)), dma((NX, 2)), dma((4,)), dma((4,)), dma((NY,)), dma((NY,)), dma((NX,)), dma((NX,)),
        ],
        compiler_params=pltpu.CompilerParams(
            collective_id=0, has_side_effects=True, vmem_limit_bytes=40 * 1024 * 1024
        ),
    )(
        *(
            pltpu.with_memory_space_constraint(a, pltpu.HBM)
            for a in (inputs, gain, w_in, pre_act, grad_act)
        )
    )
    return grad_input, grad_w_in, grad_gain


def solution(mesh):
    return jax.shard_map(
        shards,
        mesh=mesh,
        in_specs=(
            P(("dp", "row"), "col"),
            P("row"),
            P("row", "col"),
            P(("dp", "row"), "col"),
            P(("dp", "row"), "col"),
        ),
        out_specs=(P(("dp", "col"), "row"), P("row", "col"), P("row")),
        check_vma=False,
    )
```

```python
import math

import jax
import jax.numpy as jnp
from jax import lax
from jax.experimental import pallas as pl
from jax.experimental.pallas import tpu as pltpu
from jax.sharding import PartitionSpec as P

MESH = pl.DeviceIdType.MESH
EPSILON = 1e-06
ROWS = 128
FEAT = 384
UNITS = 1536
NZ, NX, NY = 8, 4, 8
FEATURES = 6144.0
CH = 2
CROWS = ROWS // CH
F32 = jnp.float32
BF16 = jnp.bfloat16
HIGH = lax.Precision.HIGHEST


def gelu_slope(values):
    coeff = math.sqrt(2.0 / math.pi)
    inner = coeff * (values + 0.044715 * values * values * values)
    tangent = jnp.tanh(inner)
    return 0.5 * (1.0 + tangent) + 0.5 * values * (1.0 - tangent * tangent) * coeff * (
        1.0 + 3.0 * 0.044715 * values * values
    )


def kernel(
    x_in, gain_in, w_in, pre_in, ga_in,
    gi_ref, gw_ref, gg_ref,
    x_ref, gain_ref, w_ref, pre_ref, ga_ref, load,
    act, hid, acc, wt, part, rx, own, ty, ry, xin, normed, st1, st2, stot, stin, gy, gx,
    xt_send, xt_recv, sin_send, sin_recv, act_recv, ring_send, sib_send, dp_send,
    h_recv, hy_send, hx_send, s1_send, s1_recv, s2_send, s2_recv,
    rx_send, rx_recv, ry_send, ry_recv, gy_send, gy_recv, gx_send, gx_recv,
):
    d, r, c = lax.axis_index("dp"), lax.axis_index("row"), lax.axis_index("col")
    z, k = r // 2, r % 2
    x, y = c // 4, c % 4
    yy = d * 4 + y

    def at(dp=None, row=None, col=None):
        return {
            "dp": d if dp is None else dp,
            "row": r if row is None else row,
            "col": c if col is None else col,
        }

    def at_z(zz):
        return at(row=zz * 2 + k)

    def at_y(big):
        return at(dp=big // 4, col=x * 4 + big % 4)

    def at_x(xx):
        return at(col=xx * 4 + y)

    def remote(src, dst, send, recv, device):
        return pltpu.make_async_remote_copy(
            src_ref=src, dst_ref=dst, send_sem=send, recv_sem=recv,
            device_id=device, device_id_type=MESH,
        )

    sibling = at(row=z * 2 + 1 - k)
    zm = lambda s: (z + s + NZ) % NZ
    ym = lambda s: (yy + s + NY) % NY
    xm = lambda s: (x + s + NX) % NX

    loads = [
        pltpu.make_async_copy(src, dst, load.at[i])
        for i, (src, dst) in enumerate(
            ((pre_in, pre_ref), (ga_in, ga_ref), (x_in, x_ref), (gain_in, gain_ref), (w_in, w_ref))
        )
    ]
    for copy in loads:
        copy.start()

    barrier = pltpu.get_barrier_semaphore()

    def greet(device):
        pl.semaphore_signal(barrier, inc=1, device_id=device, device_id_type=MESH)

    @pl.loop(1, 16)
    def _(i):
        greet(at(row=(r + i) % 16))

    @pl.loop(1, 16)
    def _(i):
        greet(at(col=(c + i) % 16))

    @pl.loop(0, 4)
    def _(i):
        greet(at(dp=1 - d, col=x * 4 + i))

    @pl.when(r != c)
    def _():
        greet(at(row=c, col=r))

    loads[0].wait()
    loads[1].wait()

    @pl.loop(0, ROWS // 16)
    def _(i):
        here = pl.ds(pl.multiple_of(i * 16, 16), 16)
        there = pl.ds(pl.multiple_of(k * ROWS + i * 16, 16), 16)
        slopes = gelu_slope(pre_ref[here, :].astype(F32))
        act[0, z, there, :] = (ga_ref[here, :].astype(F32) * slopes).astype(BF16)

    for copy in loads[2:]:
        copy.wait()
    gain = gain_ref[...].reshape(1, FEAT)

    @pl.when(r != c)
    def _():
        pl.semaphore_wait(barrier, 15 + 15 + 4 + 1)

    @pl.when(r == c)
    def _():
        pl.semaphore_wait(barrier, 15 + 15 + 4)

    swap = remote(x_ref, xin, xt_send, xt_recv, at(row=c, col=r))

    @pl.when(r != c)
    def _():
        swap.start()

    @pl.when(r == c)
    def _():
        xin[...] = x_ref[...]

    def act_piece(ph, zz, kk, ch):
        return act.at[ph, zz, pl.ds(pl.multiple_of(kk * ROWS + ch * CROWS, CROWS), CROWS), :]

    def ring_copy(ph, zz, ch, to, slot):
        piece = act_piece(ph, zz, k, ch)
        return remote(
            piece, piece, ring_send.at[ph, slot, ch], act_recv.at[ph, zz, k, ch], at_z(to)
        )

    def sib_copy(ph, zz, kk, ch, slot):
        piece = act_piece(ph, zz, kk, ch)
        return remote(
            piece, piece, sib_send.at[ph, slot, ch], act_recv.at[ph, zz, kk, ch], sibling
        )

    def dp_copy(ch):
        return remote(
            act_piece(0, z, k, ch), act_piece(1, z, k, ch),
            dp_send.at[ch], act_recv.at[1, z, k, ch], at(dp=1 - d),
        )

    def wait_act(ph, zz, kk, ch):
        sib_copy(ph, zz, kk, ch, 0).wait_recv()

    def start_own(ph, ch):
        ring_copy(ph, z, ch, zm(1), 0).start()
        ring_copy(ph, z, ch, zm(-1), 1).start()
        sib_copy(ph, z, k, ch, 0).start()

    for ch in range(CH):
        start_own(0, ch)
        if ch == 0:
            dp_copy(ch).start()

    def ring_step(ph, s, ch):
        if s < 4:
            for sign, slot in ((-1, 0), (1, 1)):
                zz = zm(sign * s)
                wait_act(ph, zz, k, ch)
                if s < 3:
                    ring_copy(ph, zz, ch, zm(-sign), 2 * s + slot).start()
                sib_copy(ph, zz, k, ch, 2 * s - 1 + slot).start()
            if s == 3:
                sign = 2 * k - 1
                ring_copy(ph, zm(sign * 3), ch, zm(-sign), 6).start()
        else:
            zz = zm(4)
            wait_act(ph, zz, k, ch)
            sib_copy(ph, zz, k, ch, 7).start()

    def wait_sibling(ph, zz):
        for ch in range(CH):
            wait_act(ph, zz, 1 - k, ch)

    ones = jnp.ones((8, FEAT), F32)
    first_row = lax.broadcasted_iota(jnp.int32, (8, ROWS), 0) == 0

    def row_pair(a, b):
        dims = (((1,), (1,)), ((), ()))
        sum_a = lax.dot_general(ones, a, dims, precision=HIGH, preferred_element_type=F32)
        sum_b = lax.dot_general(ones, b, dims, precision=HIGH, preferred_element_type=F32)
        return jnp.where(first_row, sum_a, sum_b)[0:2]

    def stat_peer(axis, i):
        return at(row=(r + i) % 16) if axis == "row" else at(col=(c + i) % 16)

    def stat_copy(buf, send, recv, axis, i):
        me = r if axis == "row" else c
        return remote(buf.at[me], buf.at[me], send.at[i], recv.at[me], stat_peer(axis, i))

    def stat_start(buf, send, recv, axis):
        @pl.loop(1, 16)
        def _(i):
            stat_copy(buf, send, recv, axis, i).start()

    def stat_finish(buf, send, recv, axis):
        @pl.loop(1, 16)
        def _(i):
            other = ((r if axis == "row" else c) + i) % 16
            remote(buf.at[other], buf.at[other], send.at[i], recv.at[other], sibling).wait_recv()

        total = buf[0]
        for i in range(1, 16):
            total = total + buf[i]
        return total

    def columns_of(total):
        column = jnp.concatenate([total, jnp.zeros((ROWS - 2, ROWS), F32)], axis=0).T / FEATURES
        return column[:, 0:1], column[:, 1:2]

    values = x_ref[...].astype(F32)
    st1[c] = row_pair(values, values * values)
    stat_start(st1, s1_send, s1_recv, "col")
    total_copy = remote(stot, stin, sin_send, sin_recv, at(row=c, col=r))

    @pl.loop(0, UNITS // 128)
    def _(i):
        span = pl.ds(pl.multiple_of(i * 128, 128), 128)
        wt[span, :] = w_ref[:, span].T

    def rx_copy(zz, i):
        half = pl.ds(pl.multiple_of((zz % 2) * 256, 256), 256)
        return remote(
            part.at[zz], rx.at[x, half], rx_send.at[i], rx_recv.at[x, zz % 2], at_x(zz // 2)
        )

    def grad_hidden_part(s, i):
        zz = zm(s)
        wait_sibling(0, zz)
        part[zz] = jnp.dot(act[0, zz], wt[...], preferred_element_type=F32).astype(BF16)

        @pl.when(zz // 2 != x)
        def _():
            rx_copy(zz, i).start()

    def hid_copy(block, device, send):
        return remote(hid.at[block], hid.at[block], send, h_recv.at[block], device)

    def hid_block(big, xx):
        return (big // 4) * 16 + xx * 4 + big % 4

    def hid_to_x(big):
        block = hid_block(big, x)
        hid_copy(block, at_x(xm(1)), hx_send.at[3 * big]).start()
        hid_copy(block, at_x(xm(-1)), hx_send.at[3 * big + 1]).start()

    def wait_hid(block):
        hid_copy(block, sibling, hx_send.at[0]).wait_recv()

    def hid_arrived(big):
        wait_hid(hid_block(big, x))

        @pl.when(big // 4 == d)
        def _():
            hid_to_x(big)

    def hid_y_step(s):
        if s < 4:
            for sign, slot in ((-1, 0), (1, 1)):
                big = ym(sign * s)
                hid_arrived(big)
                if s < 3:
                    hid_copy(hid_block(big, x), at_y(ym(-sign)), hy_send.at[2 * s + slot]).start()
            if s == 3:
                sign = 2 * k - 1
                hid_copy(hid_block(ym(3 * sign), x), at_y(ym(-sign)), hy_send.at[6]).start()
        else:
            hid_arrived(ym(4))

    def hid_others():
        for i in range(4):
            hid_to_x((1 - d) * 4 + (y + i) % 4)

    def hid_x_step(ph, i):
        big = (d if ph == 0 else 1 - d) * 4 + (y + i) % 4
        wait_hid(hid_block(big, xm(1)))
        wait_hid(hid_block(big, xm(-1)))
        sign = 2 * k - 1
        hid_copy(hid_block(big, xm(sign)), at_x(xm(-sign)), hx_send.at[3 * big + 2]).start()

    def hid_ready(ph):
        @pl.loop(0, 4)
        def _(i):
            wait_hid(hid_block((d if ph == 0 else 1 - d) * 4 + i, xm(2)))

    def project(ph, zz, first=False, last=False):
        replica = d if ph == 0 else 1 - d
        lhs = jnp.concatenate(
            [hid[replica * 16 + 2 * zz], hid[replica * 16 + 2 * zz + 1]], axis=1
        )

        @pl.loop(0, UNITS // 512)
        def _(i):
            span = pl.ds(pl.multiple_of(i * 512, 512), 512)
            term = jnp.dot(lhs, act[ph, zz, :, span], preferred_element_type=F32)
            out = gw_ref if ph == 0 else acc
            if first:
                out[:, span] = term
            elif last:
                gw_ref[:, span] = gw_ref[:, span] + (acc[:, span] + term)
            else:
                out[:, span] = out[:, span] + term

    def x_sum(yq):
        rows = pl.ds(pl.multiple_of(yq * ROWS, ROWS), ROWS)
        inner = pl.ds(pl.multiple_of((yq % 2) * ROWS, ROWS), ROWS)
        total = part[2 * x + yq // 2, inner, :].astype(F32)
        for i in range(1, NX):
            total = total + rx[xm(i), rows, :].astype(F32)
        return total

    def ry_copy(i):
        to = (y + i) % 4
        return remote(ty.at[to], ry.at[y], ry_send.at[i], ry_recv.at[y], at(col=x * 4 + to))

    def gain_sum(buf, count, me, send, recv, device_of):
        @pl.loop(1, count)
        def _(i):
            remote(buf.at[me], buf.at[me], send.at[i], recv.at[me], device_of((me + i) % count)).start()

    def gain_wait(buf, count, me, send, recv):
        @pl.loop(1, count)
        def _(i):
            other = (me + i) % count
            remote(buf.at[other], buf.at[other], send.at[i], recv.at[other], sibling).wait_recv()

        total = buf[0]
        for i in range(1, count):
            total = total + buf[i]
        return total

    def gain_drain(buf, count, me, send, recv):
        @pl.loop(1, count)
        def _(i):
            remote(buf.at[me], buf.at[me], send.at[i], recv.at[me], sibling).wait_send()

    grad_hidden_part(0, 0)
    stot[...] = stat_finish(st1, s1_send, s1_recv, "col")

    @pl.when(r != c)
    def _():
        total_copy.start()

    @pl.when(r == c)
    def _():
        stin[...] = stot[...]

    ring_step(0, 1, 0)
    ring_step(0, 1, 1)

    @pl.when(r != c)
    def _():
        swap.wait_recv()
        total_copy.wait_recv()

    row_mean, square_mean = columns_of(stin[...])
    variance = square_mean - row_mean * row_mean
    inv_std = lax.rsqrt(variance + EPSILON)
    normed[...] = (xin[...].astype(F32) - row_mean) * inv_std
    hid[d * 16 + c] = (normed[...] * gain).T.astype(BF16)
    for sign, slot in ((1, 0), (-1, 1)):
        hid_copy(hid_block(yy, x), at_y(ym(sign)), hy_send.at[slot]).start()
    hid_to_x(yy)
    dp_copy(1).start()

    grad_hidden_part(1, 1)
    grad_hidden_part(-1, 2)
    ring_step(0, 2, 0)
    hid_y_step(1)
    hid_x_step(0, 0)
    ring_step(0, 2, 1)
    grad_hidden_part(2, 3)
    grad_hidden_part(-2, 4)
    hid_y_step(2)
    ring_step(0, 3, 0)
    hid_y_step(3)
    ring_step(0, 3, 1)
    for ch in range(CH):
        wait_act(1, z, k, ch)
        start_own(1, ch)
    grad_hidden_part(3, 5)
    grad_hidden_part(-3, 6)
    ring_step(0, 4, 0)
    hid_y_step(4)
    hid_x_step(0, 1)
    hid_x_step(0, 2)
    hid_x_step(0, 3)
    ring_step(1, 1, 0)
    ring_step(0, 4, 1)
    grad_hidden_part(4, 7)
    hid_others()
    hid_ready(0)
    ring_step(1, 1, 1)
    for s in (0, 1, -1, 2, -2, 3):
        project(0, zm(s), first=s == 0)
    ring_step(1, 2, 0)

    for half in range(2):
        @pl.loop(1, NX)
        def _(i):
            other = (x + i) % NX
            rows = pl.ds(half * 256, 256)
            remote(
                part.at[0], rx.at[other, rows], rx_send.at[0], rx_recv.at[other, half], sibling
            ).wait_recv()

    for i in range(1, 4):
        ty[(y + i) % 4] = x_sum((y + i) % 4).astype(BF16)
        ry_copy(i).start()
    own[...] = x_sum(y)
    hid_x_step(1, 0)
    hid_x_step(1, 1)
    ring_step(1, 2, 1)
    hid_x_step(1, 2)
    hid_x_step(1, 3)
    for s in (-3, 4):
        project(0, zm(s))
    ring_step(1, 3, 0)

    for i in range(1, 4):
        other = (y + i) % 4
        remote(ty.at[0], ry.at[other], ry_send.at[0], ry_recv.at[other], sibling).wait_recv()
    grad_hidden = own[...]
    for i in range(1, 4):
        grad_hidden = grad_hidden + ry[(y + i) % 4].astype(F32)

    scaled = grad_hidden * gain
    own_normed = normed[...]
    gy[yy] = jnp.sum(grad_hidden * own_normed, axis=0, keepdims=True)
    gain_sum(gy, NY, yy, gy_send, gy_recv, at_y)
    st2[r] = row_pair(scaled, scaled * own_normed)
    stat_start(st2, s2_send, s2_recv, "row")
    own[...] = scaled
    ring_step(1, 3, 1)
    hid_ready(1)
    wait_sibling(1, z)
    project(1, z, first=True)
    for s in (1, -1):
        wait_sibling(1, zm(s))
        project(1, zm(s))
    ring_step(1, 4, 0)
    gx[x] = gain_wait(gy, NY, yy, gy_send, gy_recv)
    gain_sum(gx, NX, x, gx_send, gx_recv, at_x)
    for s in (2, -2):
        wait_sibling(1, zm(s))
        project(1, zm(s))
    first_mean, second_mean = columns_of(stat_finish(st2, s2_send, s2_recv, "row"))
    gi_ref[...] = (
        inv_std * (own[...] - first_mean - normed[...] * second_mean)
    ).astype(BF16)
    ring_step(1, 4, 1)
    for s in (3, -3):
        wait_sibling(1, zm(s))
        project(1, zm(s))
    wait_sibling(1, zm(4))
    project(1, zm(4), last=True)
    gg_ref[...] = gain_wait(gx, NX, x, gx_send, gx_recv)[0]

    @pl.when(r != c)
    def _():
        swap.wait_send()
        total_copy.wait_send()

    for ch in range(CH):
        dp_copy(ch).wait_send()

    for ph in range(2):
        @pl.loop(0, 7)
        def _(slot):
            for ch in range(CH):
                remote(
                    act_piece(ph, z, k, ch), act_piece(ph, z, k, ch),
                    ring_send.at[ph, slot, ch], act_recv.at[ph, z, k, ch], sibling,
                ).wait_send()

        @pl.loop(0, 8)
        def _(slot):
            for ch in range(CH):
                sib_copy(ph, z, k, ch, slot).wait_send()

    @pl.loop(0, 7)
    def _(slot):
        hid_copy(0, sibling, hy_send.at[slot]).wait_send()

    @pl.loop(0, 24)
    def _(slot):
        hid_copy(0, sibling, hx_send.at[slot]).wait_send()

    for i, step in enumerate((0, 1, -1, 2, -2, 3, -3, 4)):
        @pl.when(zm(step) // 2 != x)
        def _():
            rx_copy(zm(step), i).wait_send()

    for i in range(1, 4):
        ry_copy(i).wait_send()

    for buf, send, recv, axis in ((st1, s1_send, s1_recv, "col"), (st2, s2_send, s2_recv, "row")):
        @pl.loop(1, 16)
        def _(i):
            stat_copy(buf, send, recv, axis, i).wait_send()

    gain_drain(gy, NY, yy, gy_send, gy_recv)
    gain_drain(gx, NX, x, gx_send, gx_recv)


def shards(inputs, gain, w_in, pre_act, grad_act):
    dma = pltpu.SemaphoreType.DMA
    grad_input, grad_w_in, grad_gain = pl.pallas_call(
        kernel,
        out_shape=(
            jax.ShapeDtypeStruct((ROWS, FEAT), BF16),
            pltpu.VMEM((FEAT, UNITS), F32),
            jax.ShapeDtypeStruct((FEAT,), F32),
        ),
        in_specs=[pl.BlockSpec(memory_space=pltpu.HBM)] * 5,
        out_specs=(pl.BlockSpec(memory_space=pltpu.VMEM),) * 3,
        scratch_shapes=[
            pltpu.VMEM((ROWS, FEAT), BF16),
            pltpu.VMEM((FEAT,), F32),
            pltpu.VMEM((FEAT, UNITS), BF16),
            pltpu.VMEM((ROWS, UNITS), BF16),
            pltpu.VMEM((ROWS, UNITS), BF16),
            dma((5,)),
            pltpu.VMEM((2, NZ, 2 * ROWS, UNITS), BF16),
            pltpu.VMEM((32, FEAT, ROWS), BF16),
            pltpu.VMEM((FEAT, UNITS), F32),
            pltpu.VMEM((UNITS, FEAT), BF16),
            pltpu.VMEM((NZ, 2 * ROWS, FEAT), BF16),
            pltpu.VMEM((NX, 4 * ROWS, FEAT), BF16),
            pltpu.VMEM((ROWS, FEAT), F32),
            pltpu.VMEM((4, ROWS, FEAT), BF16),
            pltpu.VMEM((4, ROWS, FEAT), BF16),
            pltpu.VMEM((ROWS, FEAT), BF16),
            pltpu.VMEM((ROWS, FEAT), F32),
            pltpu.VMEM((16, 2, ROWS), F32),
            pltpu.VMEM((16, 2, ROWS), F32),
            pltpu.VMEM((2, ROWS), F32),
            pltpu.VMEM((2, ROWS), F32),
            pltpu.VMEM((NY, 1, FEAT), F32),
            pltpu.VMEM((NX, 1, FEAT), F32),
            dma, dma, dma, dma, dma((2, NZ, 2, CH)), dma((2, 7, CH)), dma((2, 8, CH)), dma((CH,)),
            dma((32,)), dma((7,)), dma((24,)), dma((16,)), dma((16,)), dma((16,)), dma((16,)),
            dma((8,)), dma((NX, 2)), dma((4,)), dma((4,)), dma((NY,)), dma((NY,)), dma((NX,)), dma((NX,)),
        ],
        compiler_params=pltpu.CompilerParams(
            collective_id=0, has_side_effects=True, vmem_limit_bytes=40 * 1024 * 1024
        ),
    )(
        *(
            pltpu.with_memory_space_constraint(a, pltpu.HBM)
            for a in (inputs, gain, w_in, pre_act, grad_act)
        )
    )
    return grad_input, grad_w_in, grad_gain


def solution(mesh):
    return jax.shard_map(
        shards,
        mesh=mesh,
        in_specs=(
            P(("dp", "row"), "col"),
            P("row"),
            P("row", "col"),
            P(("dp", "row"), "col"),
            P(("dp", "row"), "col"),
        ),
        out_specs=(P(("dp", "col"), "row"), P("row", "col"), P("row")),
        check_vma=False,
    )
```

```python
import math

import jax
import jax.numpy as jnp
from jax import lax
from jax.experimental import pallas as pl
from jax.experimental.pallas import tpu as pltpu
from jax.sharding import PartitionSpec as P

MESH = pl.DeviceIdType.MESH
EPSILON = 1e-06
ROWS = 128
FEAT = 384
UNITS = 1536
NZ, NX, NY = 8, 4, 8
FEATURES = 6144.0
CH = 2
CROWS = ROWS // CH
F32 = jnp.float32
BF16 = jnp.bfloat16
HIGH = lax.Precision.HIGHEST


def gelu_slope(values):
    coeff = math.sqrt(2.0 / math.pi)
    inner = coeff * (values + 0.044715 * values * values * values)
    tangent = jnp.tanh(inner)
    return 0.5 * (1.0 + tangent) + 0.5 * values * (1.0 - tangent * tangent) * coeff * (
        1.0 + 3.0 * 0.044715 * values * values
    )


def kernel(
    x_in, gain_in, w_in, pre_in, ga_in,
    gi_ref, gw_ref, gg_ref,
    x_ref, gain_ref, w_ref, pre_ref, ga_ref, load,
    act, hid, acc, wt, part, rx, own, ty, ry, xin, normed, st1, st2, stot, stin, gy, gx,
    xt_send, xt_recv, sin_send, sin_recv, act_recv, ring_send, sib_send, dp_send,
    h_recv, hy_send, hx_send, s1_send, s1_recv, s2_send, s2_recv,
    rx_send, rx_recv, ry_send, ry_recv, gy_send, gy_recv, gx_send, gx_recv,
):
    d, r, c = lax.axis_index("dp"), lax.axis_index("row"), lax.axis_index("col")
    z, k = r // 2, r % 2
    x, y = c // 4, c % 4
    yy = d * 4 + y

    def at(dp=None, row=None, col=None):
        return {
            "dp": d if dp is None else dp,
            "row": r if row is None else row,
            "col": c if col is None else col,
        }

    def at_z(zz):
        return at(row=zz * 2 + k)

    def at_y(big):
        return at(dp=big // 4, col=x * 4 + big % 4)

    def at_x(xx):
        return at(col=xx * 4 + y)

    def remote(src, dst, send, recv, device):
        return pltpu.make_async_remote_copy(
            src_ref=src, dst_ref=dst, send_sem=send, recv_sem=recv,
            device_id=device, device_id_type=MESH,
        )

    sibling = at(row=z * 2 + 1 - k)
    zm = lambda s: (z + s + NZ) % NZ
    ym = lambda s: (yy + s + NY) % NY
    xm = lambda s: (x + s + NX) % NX

    loads = [
        pltpu.make_async_copy(src, dst, load.at[i])
        for i, (src, dst) in enumerate(
            ((pre_in, pre_ref), (ga_in, ga_ref), (x_in, x_ref), (gain_in, gain_ref), (w_in, w_ref))
        )
    ]
    for copy in loads:
        copy.start()

    barrier = pltpu.get_barrier_semaphore()

    def greet(device):
        pl.semaphore_signal(barrier, inc=1, device_id=device, device_id_type=MESH)

    @pl.loop(1, 16)
    def _(i):
        greet(at(row=(r + i) % 16))

    @pl.loop(1, 16)
    def _(i):
        greet(at(col=(c + i) % 16))

    @pl.loop(0, 4)
    def _(i):
        greet(at(dp=1 - d, col=x * 4 + i))

    @pl.when(r != c)
    def _():
        greet(at(row=c, col=r))

    loads[0].wait()
    loads[1].wait()

    @pl.loop(0, ROWS // 16)
    def _(i):
        here = pl.ds(pl.multiple_of(i * 16, 16), 16)
        there = pl.ds(pl.multiple_of(k * ROWS + i * 16, 16), 16)
        slopes = gelu_slope(pre_ref[here, :].astype(F32))
        act[0, z, there, :] = (ga_ref[here, :].astype(F32) * slopes).astype(BF16)

    for copy in loads[2:]:
        copy.wait()
    gain = gain_ref[...].reshape(1, FEAT)

    @pl.when(r != c)
    def _():
        pl.semaphore_wait(barrier, 15 + 15 + 4 + 1)

    @pl.when(r == c)
    def _():
        pl.semaphore_wait(barrier, 15 + 15 + 4)

    swap = remote(x_ref, xin, xt_send, xt_recv, at(row=c, col=r))

    @pl.when(r != c)
    def _():
        swap.start()

    @pl.when(r == c)
    def _():
        xin[...] = x_ref[...]

    def act_piece(ph, zz, kk, ch):
        return act.at[ph, zz, pl.ds(pl.multiple_of(kk * ROWS + ch * CROWS, CROWS), CROWS), :]

    def ring_copy(ph, zz, ch, to, slot):
        piece = act_piece(ph, zz, k, ch)
        return remote(
            piece, piece, ring_send.at[ph, slot, ch], act_recv.at[ph, zz, k, ch], at_z(to)
        )

    def sib_copy(ph, zz, kk, ch, slot):
        piece = act_piece(ph, zz, kk, ch)
        return remote(
            piece, piece, sib_send.at[ph, slot, ch], act_recv.at[ph, zz, kk, ch], sibling
        )

    def dp_copy(ch):
        return remote(
            act_piece(0, z, k, ch), act_piece(1, z, k, ch),
            dp_send.at[ch], act_recv.at[1, z, k, ch], at(dp=1 - d),
        )

    def wait_act(ph, zz, kk, ch):
        sib_copy(ph, zz, kk, ch, 0).wait_recv()

    def start_own(ph, ch):
        ring_copy(ph, z, ch, zm(1), 0).start()
        ring_copy(ph, z, ch, zm(-1), 1).start()
        sib_copy(ph, z, k, ch, 0).start()

    for ch in range(CH):
        start_own(0, ch)
        if ch == 0:
            dp_copy(ch).start()

    def ring_step(ph, s, ch):
        if s < 4:
            for sign, slot in ((-1, 0), (1, 1)):
                zz = zm(sign * s)
                wait_act(ph, zz, k, ch)
                if s < 3:
                    ring_copy(ph, zz, ch, zm(-sign), 2 * s + slot).start()
                sib_copy(ph, zz, k, ch, 2 * s - 1 + slot).start()
            if s == 3:
                sign = 2 * k - 1
                ring_copy(ph, zm(sign * 3), ch, zm(-sign), 6).start()
        else:
            zz = zm(4)
            wait_act(ph, zz, k, ch)
            sib_copy(ph, zz, k, ch, 7).start()

    def wait_sibling(ph, zz):
        for ch in range(CH):
            wait_act(ph, zz, 1 - k, ch)

    ones = jnp.ones((8, FEAT), F32)
    first_row = lax.broadcasted_iota(jnp.int32, (8, ROWS), 0) == 0

    def row_pair(a, b):
        dims = (((1,), (1,)), ((), ()))
        sum_a = lax.dot_general(ones, a, dims, precision=HIGH, preferred_element_type=F32)
        sum_b = lax.dot_general(ones, b, dims, precision=HIGH, preferred_element_type=F32)
        return jnp.where(first_row, sum_a, sum_b)[0:2]

    def stat_peer(axis, i):
        return at(row=(r + i) % 16) if axis == "row" else at(col=(c + i) % 16)

    def stat_copy(buf, send, recv, axis, i):
        me = r if axis == "row" else c
        return remote(buf.at[me], buf.at[me], send.at[i], recv.at[me], stat_peer(axis, i))

    def stat_start(buf, send, recv, axis):
        @pl.loop(1, 16)
        def _(i):
            stat_copy(buf, send, recv, axis, i).start()

    def stat_finish(buf, send, recv, axis):
        @pl.loop(1, 16)
        def _(i):
            other = ((r if axis == "row" else c) + i) % 16
            remote(buf.at[other], buf.at[other], send.at[i], recv.at[other], sibling).wait_recv()

        total = buf[0]
        for i in range(1, 16):
            total = total + buf[i]
        return total

    def columns_of(total):
        column = jnp.concatenate([total, jnp.zeros((ROWS - 2, ROWS), F32)], axis=0).T / FEATURES
        return column[:, 0:1], column[:, 1:2]

    values = x_ref[...].astype(F32)
    st1[c] = row_pair(values, values * values)
    stat_start(st1, s1_send, s1_recv, "col")
    total_copy = remote(stot, stin, sin_send, sin_recv, at(row=c, col=r))

    @pl.loop(0, UNITS // 128)
    def _(i):
        span = pl.ds(pl.multiple_of(i * 128, 128), 128)
        wt[span, :] = w_ref[:, span].T

    def rx_copy(zz, i):
        half = pl.ds(pl.multiple_of((zz % 2) * 256, 256), 256)
        return remote(
            part.at[zz], rx.at[x, half], rx_send.at[i], rx_recv.at[x, zz % 2], at_x(zz // 2)
        )

    def grad_hidden_part(s, i):
        zz = zm(s)
        wait_sibling(0, zz)
        part[zz] = jnp.dot(act[0, zz], wt[...], preferred_element_type=F32).astype(BF16)

        @pl.when(zz // 2 != x)
        def _():
            rx_copy(zz, i).start()

    def hid_copy(block, device, send):
        return remote(hid.at[block], hid.at[block], send, h_recv.at[block], device)

    def hid_block(big, xx):
        return (big // 4) * 16 + xx * 4 + big % 4

    def hid_to_x(big):
        block = hid_block(big, x)
        hid_copy(block, at_x(xm(1)), hx_send.at[3 * big]).start()
        hid_copy(block, at_x(xm(-1)), hx_send.at[3 * big + 1]).start()

    def wait_hid(block):
        hid_copy(block, sibling, hx_send.at[0]).wait_recv()

    def hid_arrived(big):
        wait_hid(hid_block(big, x))

        @pl.when(big // 4 == d)
        def _():
            hid_to_x(big)

    def hid_y_step(s):
        if s < 4:
            for sign, slot in ((-1, 0), (1, 1)):
                big = ym(sign * s)
                hid_arrived(big)
                if s < 3:
                    hid_copy(hid_block(big, x), at_y(ym(-sign)), hy_send.at[2 * s + slot]).start()
            if s == 3:
                sign = 2 * k - 1
                hid_copy(hid_block(ym(3 * sign), x), at_y(ym(-sign)), hy_send.at[6]).start()
        else:
            hid_arrived(ym(4))

    def hid_others():
        for i in range(4):
            hid_to_x((1 - d) * 4 + (y + i) % 4)

    def hid_x_step(ph, i):
        big = (d if ph == 0 else 1 - d) * 4 + (y + i) % 4
        wait_hid(hid_block(big, xm(1)))
        wait_hid(hid_block(big, xm(-1)))
        sign = 2 * k - 1
        hid_copy(hid_block(big, xm(sign)), at_x(xm(-sign)), hx_send.at[3 * big + 2]).start()

    def hid_ready(ph):
        @pl.loop(0, 4)
        def _(i):
            wait_hid(hid_block((d if ph == 0 else 1 - d) * 4 + i, xm(2)))

    def project(ph, zz, first=False, last=False):
        replica = d if ph == 0 else 1 - d
        lhs = jnp.concatenate(
            [hid[replica * 16 + 2 * zz], hid[replica * 16 + 2 * zz + 1]], axis=1
        )

        @pl.loop(0, UNITS // 512)
        def _(i):
            span = pl.ds(pl.multiple_of(i * 512, 512), 512)
            term = jnp.dot(lhs, act[ph, zz, :, span], preferred_element_type=F32)
            out = gw_ref if ph == 0 else acc
            if first:
                out[:, span] = term
            elif last:
                gw_ref[:, span] = gw_ref[:, span] + (acc[:, span] + term)
            else:
                out[:, span] = out[:, span] + term

    def x_sum(yq):
        rows = pl.ds(pl.multiple_of(yq * ROWS, ROWS), ROWS)
        inner = pl.ds(pl.multiple_of((yq % 2) * ROWS, ROWS), ROWS)
        total = part[2 * x + yq // 2, inner, :].astype(F32)
        for i in range(1, NX):
            total = total + rx[xm(i), rows, :].astype(F32)
        return total

    def ry_copy(i):
        to = (y + i) % 4
        return remote(ty.at[to], ry.at[y], ry_send.at[i], ry_recv.at[y], at(col=x * 4 + to))

    def gain_sum(buf, count, me, send, recv, device_of):
        @pl.loop(1, count)
        def _(i):
            remote(buf.at[me], buf.at[me], send.at[i], recv.at[me], device_of((me + i) % count)).start()

    def gain_wait(buf, count, me, send, recv):
        @pl.loop(1, count)
        def _(i):
            other = (me + i) % count
            remote(buf.at[other], buf.at[other], send.at[i], recv.at[other], sibling).wait_recv()

        total = buf[0]
        for i in range(1, count):
            total = total + buf[i]
        return total

    def gain_drain(buf, count, me, send, recv):
        @pl.loop(1, count)
        def _(i):
            remote(buf.at[me], buf.at[me], send.at[i], recv.at[me], sibling).wait_send()

    grad_hidden_part(0, 0)
    stot[...] = stat_finish(st1, s1_send, s1_recv, "col")

    @pl.when(r != c)
    def _():
        total_copy.start()

    @pl.when(r == c)
    def _():
        stin[...] = stot[...]

    ring_step(0, 1, 0)
    ring_step(0, 1, 1)

    @pl.when(r != c)
    def _():
        swap.wait_recv()
        total_copy.wait_recv()

    row_mean, square_mean = columns_of(stin[...])
    variance = square_mean - row_mean * row_mean
    inv_std = lax.rsqrt(variance + EPSILON)
    normed[...] = (xin[...].astype(F32) - row_mean) * inv_std
    hid[d * 16 + c] = (normed[...] * gain).T.astype(BF16)
    for sign, slot in ((1, 0), (-1, 1)):
        hid_copy(hid_block(yy, x), at_y(ym(sign)), hy_send.at[slot]).start()
    hid_to_x(yy)
    dp_copy(1).start()

    grad_hidden_part(1, 1)
    grad_hidden_part(-1, 2)
    ring_step(0, 2, 0)
    hid_y_step(1)
    hid_x_step(0, 0)
    ring_step(0, 2, 1)
    grad_hidden_part(2, 3)
    grad_hidden_part(-2, 4)
    hid_y_step(2)
    ring_step(0, 3, 0)
    hid_y_step(3)
    ring_step(0, 3, 1)
    for ch in range(CH):
        wait_act(1, z, k, ch)
        start_own(1, ch)
    grad_hidden_part(3, 5)
    grad_hidden_part(-3, 6)
    ring_step(0, 4, 0)
    hid_y_step(4)
    hid_x_step(0, 1)
    hid_x_step(0, 2)
    hid_x_step(0, 3)
    ring_step(1, 1, 0)
    ring_step(0, 4, 1)
    grad_hidden_part(4, 7)
    hid_others()
    hid_ready(0)
    ring_step(1, 1, 1)
    for s in (0, 1, -1, 2, -2, 3):
        project(0, zm(s), first=s == 0)
    ring_step(1, 2, 0)

    for half in range(2):
        @pl.loop(1, NX)
        def _(i):
            other = (x + i) % NX
            rows = pl.ds(half * 256, 256)
            remote(
                part.at[0], rx.at[other, rows], rx_send.at[0], rx_recv.at[other, half], sibling
            ).wait_recv()

    for i in range(1, 4):
        ty[(y + i) % 4] = x_sum((y + i) % 4).astype(BF16)
        ry_copy(i).start()
    own[...] = x_sum(y)
    hid_x_step(1, 0)
    hid_x_step(1, 1)
    ring_step(1, 2, 1)
    hid_x_step(1, 2)
    hid_x_step(1, 3)
    for s in (-3, 4):
        project(0, zm(s))
    ring_step(1, 3, 0)

    for i in range(1, 4):
        other = (y + i) % 4
        remote(ty.at[0], ry.at[other], ry_send.at[0], ry_recv.at[other], sibling).wait_recv()
    grad_hidden = own[...]
    for i in range(1, 4):
        grad_hidden = grad_hidden + ry[(y + i) % 4].astype(F32)

    scaled = grad_hidden * gain
    own_normed = normed[...]
    gy[yy] = jnp.sum(grad_hidden * own_normed, axis=0, keepdims=True)
    gain_sum(gy, NY, yy, gy_send, gy_recv, at_y)
    st2[r] = row_pair(scaled, scaled * own_normed)
    stat_start(st2, s2_send, s2_recv, "row")
    own[...] = scaled
    ring_step(1, 3, 1)
    hid_ready(1)
    wait_sibling(1, z)
    project(1, z, first=True)
    for s in (1, -1):
        wait_sibling(1, zm(s))
        project(1, zm(s))
    gx[x] = gain_wait(gy, NY, yy, gy_send, gy_recv)
    gain_sum(gx, NX, x, gx_send, gx_recv, at_x)
    ring_step(1, 4, 0)
    for s in (2, -2):
        wait_sibling(1, zm(s))
        project(1, zm(s))
    first_mean, second_mean = columns_of(stat_finish(st2, s2_send, s2_recv, "row"))
    gi_ref[...] = (
        inv_std * (own[...] - first_mean - normed[...] * second_mean)
    ).astype(BF16)
    ring_step(1, 4, 1)
    for s in (3, -3):
        wait_sibling(1, zm(s))
        project(1, zm(s))
    wait_sibling(1, zm(4))
    project(1, zm(4), last=True)
    gg_ref[...] = gain_wait(gx, NX, x, gx_send, gx_recv)[0]

    @pl.when(r != c)
    def _():
        swap.wait_send()
        total_copy.wait_send()

    for ch in range(CH):
        dp_copy(ch).wait_send()

    for ph in range(2):
        @pl.loop(0, 7)
        def _(slot):
            for ch in range(CH):
                remote(
                    act_piece(ph, z, k, ch), act_piece(ph, z, k, ch),
                    ring_send.at[ph, slot, ch], act_recv.at[ph, z, k, ch], sibling,
                ).wait_send()

        @pl.loop(0, 8)
        def _(slot):
            for ch in range(CH):
                sib_copy(ph, z, k, ch, slot).wait_send()

    @pl.loop(0, 7)
    def _(slot):
        hid_copy(0, sibling, hy_send.at[slot]).wait_send()

    @pl.loop(0, 24)
    def _(slot):
        hid_copy(0, sibling, hx_send.at[slot]).wait_send()

    for i, step in enumerate((0, 1, -1, 2, -2, 3, -3, 4)):
        @pl.when(zm(step) // 2 != x)
        def _():
            rx_copy(zm(step), i).wait_send()

    for i in range(1, 4):
        ry_copy(i).wait_send()

    for buf, send, recv, axis in ((st1, s1_send, s1_recv, "col"), (st2, s2_send, s2_recv, "row")):
        @pl.loop(1, 16)
        def _(i):
            stat_copy(buf, send, recv, axis, i).wait_send()

    gain_drain(gy, NY, yy, gy_send, gy_recv)
    gain_drain(gx, NX, x, gx_send, gx_recv)


def shards(inputs, gain, w_in, pre_act, grad_act):
    dma = pltpu.SemaphoreType.DMA
    grad_input, grad_w_in, grad_gain = pl.pallas_call(
        kernel,
        out_shape=(
            jax.ShapeDtypeStruct((ROWS, FEAT), BF16),
            pltpu.VMEM((FEAT, UNITS), F32),
            jax.ShapeDtypeStruct((FEAT,), F32),
        ),
        in_specs=[pl.BlockSpec(memory_space=pltpu.HBM)] * 5,
        out_specs=(pl.BlockSpec(memory_space=pltpu.VMEM),) * 3,
        scratch_shapes=[
            pltpu.VMEM((ROWS, FEAT), BF16),
            pltpu.VMEM((FEAT,), F32),
            pltpu.VMEM((FEAT, UNITS), BF16),
            pltpu.VMEM((ROWS, UNITS), BF16),
            pltpu.VMEM((ROWS, UNITS), BF16),
            dma((5,)),
            pltpu.VMEM((2, NZ, 2 * ROWS, UNITS), BF16),
            pltpu.VMEM((32, FEAT, ROWS), BF16),
            pltpu.VMEM((FEAT, UNITS), F32),
            pltpu.VMEM((UNITS, FEAT), BF16),
            pltpu.VMEM((NZ, 2 * ROWS, FEAT), BF16),
            pltpu.VMEM((NX, 4 * ROWS, FEAT), BF16),
            pltpu.VMEM((ROWS, FEAT), F32),
            pltpu.VMEM((4, ROWS, FEAT), BF16),
            pltpu.VMEM((4, ROWS, FEAT), BF16),
            pltpu.VMEM((ROWS, FEAT), BF16),
            pltpu.VMEM((ROWS, FEAT), F32),
            pltpu.VMEM((16, 2, ROWS), F32),
            pltpu.VMEM((16, 2, ROWS), F32),
            pltpu.VMEM((2, ROWS), F32),
            pltpu.VMEM((2, ROWS), F32),
            pltpu.VMEM((NY, 1, FEAT), F32),
            pltpu.VMEM((NX, 1, FEAT), F32),
            dma, dma, dma, dma, dma((2, NZ, 2, CH)), dma((2, 7, CH)), dma((2, 8, CH)), dma((CH,)),
            dma((32,)), dma((7,)), dma((24,)), dma((16,)), dma((16,)), dma((16,)), dma((16,)),
            dma((8,)), dma((NX, 2)), dma((4,)), dma((4,)), dma((NY,)), dma((NY,)), dma((NX,)), dma((NX,)),
        ],
        compiler_params=pltpu.CompilerParams(
            collective_id=0, has_side_effects=True, vmem_limit_bytes=40 * 1024 * 1024
        ),
    )(
        *(
            pltpu.with_memory_space_constraint(a, pltpu.HBM)
            for a in (inputs, gain, w_in, pre_act, grad_act)
        )
    )
    return grad_input, grad_w_in, grad_gain


def solution(mesh):
    return jax.shard_map(
        shards,
        mesh=mesh,
        in_specs=(
            P(("dp", "row"), "col"),
            P("row"),
            P("row", "col"),
            P(("dp", "row"), "col"),
            P(("dp", "row"), "col"),
        ),
        out_specs=(P(("dp", "col"), "row"), P("row", "col"), P("row")),
        check_vma=False,
    )
```
